128 devices in a mesh: dp: 16 (over y, z), expert: 8 (over x, core).
Axes of the slice: x: 4, y: 4, z: 4, core: 2. Of those that a mesh axis runs over, the one named last changes fastest.
Arguments:
- tokens: bfloat16 [16384, 8192], P(('dp', 'expert')), may hold values from -6 to 6
- modality: int32 [16384], P(('dp', 'expert')), may hold values from 0 to 1, as said below
- norm_gain: float32 [2, 8192], replicated, may hold values from 0.1 to 1.9
- picks: int32 [8, 128, 8], P(None, ('dp', 'expert')), may hold values from 0 to 16383, as said below
- counts: int32 [8, 128], replicated, may hold values from 0 to 8, as said below
- router: bfloat16 [8, 8192], P('expert'), may hold values from -0.0625 to 0.0625
- gate_weight: bfloat16 [8, 8192, 4096], P('expert', None, 'dp'), may hold values from -0.0625 to 0.0625
- up_weight: bfloat16 [8, 8192, 4096], P('expert', None, 'dp'), may hold values from -0.0625 to 0.0625
- down_weight: bfloat16 [8, 4096, 8192], P('expert', 'dp'), may hold values from -0.09375 to 0.09375
Outputs:
- mixed: bfloat16 [16384, 8192], P(('dp', 'expert'))
The draws below stay inside these ranges and needn't reach their ends.
Inputs may be any that keep to these rules, and one draw needn't show every extreme that they name: `modality`: each device's 128 tokens hold at least 8 text and 8 image tokens. picks[e, s, k] names a token of device s (rows s * 128 to (s + 1) * 128 - 1); the 8 entries of one list are distinct tokens whose modality is 0 for e < 4 and 1 otherwise; only the first counts[e, s] of them are chosen, the rest is padding. For each expert and each dp index j, the counts of the devices j * 8 to (j + 1) * 8 - 1 add up to at most 32; for every expert some dp index reaches 32.
All inputs are finite; a program needn't handle non-finite values.
Results may differ from the reference program's by a relative error of at most 0.0095.
Values may be sent and summed in bfloat16 or wider, within the bound.
A program may use at most 128 MiB of HBM per device.

```python
import jax
import jax.numpy as jnp
from jax import lax

D = 8192
FFW = 4096
TOK_DEV = 128
PICK = 8
EXPERTS = 8
TOKENS = 16384
N_DP = 16
N_EXPERT = 8
DEVICES = 128


def modality_table(key):
    key = jax.random.fold_in(key, 11)
    key_first, key_second = jax.random.split(key)
    rank_table = jax.vmap(lambda subkey: jax.random.permutation(subkey, TOK_DEV))(jax.random.split(key_first, DEVICES))
    text_count = PICK + jax.random.randint(key_second, (DEVICES, 1), 0, TOK_DEV - 2 * PICK + 1)
    return (rank_table >= text_count).astype(jnp.int32)


def draw_modality(key, part):
    return modality_table(key).reshape(-1)


def draw_picks(key, part):
    flag_table = modality_table(key)
    key = jax.random.fold_in(key, 2)
    group_flag = (jnp.arange(EXPERTS) >= EXPERTS // 2).astype(jnp.int32)
    mismatch = (flag_table[None, :, :] != group_flag[:, None, None]).astype(jnp.int32)
    noise_bits = jax.random.randint(key, (EXPERTS, DEVICES, TOK_DEV), 0, 4096)
    ranking = (mismatch * 4096 + noise_bits) * TOK_DEV + jnp.arange(TOK_DEV)[None, None, :]
    ordering = jnp.argsort(ranking, axis=2, stable=True)[:, :, :PICK]
    return (ordering + jnp.arange(DEVICES)[None, :, None] * TOK_DEV).astype(jnp.int32)


def draw_counts(key, part):
    key = jax.random.fold_in(key, 5)
    key_list = jax.random.split(key, 3)
    live_most = PICK * N_EXPERT // 2
    raw_counts = jax.random.randint(key_list[0], (EXPERTS, N_DP, N_EXPERT), 0, PICK + 1)
    full_row = jax.random.randint(key_list[1], (EXPERTS, 1, 1), 0, N_DP)
    raw_counts = jnp.where(jnp.arange(N_DP)[None, :, None] == full_row, PICK, raw_counts)
    rank_table = jax.vmap(lambda subkey: jax.random.permutation(subkey, N_EXPERT))(jax.random.split(key_list[2], EXPERTS * N_DP)).reshape(EXPERTS, N_DP, N_EXPERT)
    earlier_mask = rank_table[:, :, None, :] < rank_table[:, :, :, None]
    prefix_sum = jnp.sum(jnp.where(earlier_mask, raw_counts[:, :, None, :], 0), axis=-1)
    capped_counts = jnp.minimum(raw_counts, jnp.maximum(live_most - prefix_sum, 0))
    return capped_counts.reshape(EXPERTS, DEVICES).astype(jnp.int32)


def steps_of(own_key, extent, shards, least, high):
    gain = 1.0
    for position, blocks in shards:
        draws = jax.random.uniform(jax.random.fold_in(jax.random.fold_in(own_key, 6), position), (blocks,), jnp.float32, least / len(shards), high / len(shards))
        gain = gain * jnp.repeat(jnp.exp(draws), extent[position] // blocks).reshape((-1,) + (1,) * (len(extent) - 1 - position))
    return gain


def scatter_about(stream_key, dims, width, bound, shards=(), dtype=jnp.bfloat16):
    values = width * jax.random.normal(stream_key, dims, jnp.float32)
    if shards:
        values = values * steps_of(stream_key, dims, shards, -0.22, 0.18)
    return jnp.clip(values, -bound, bound).astype(dtype)


def setup_inputs(seed: int = 0) -> dict:
    streams_of = jax.random.split(jax.random.key(seed), 10)
    return {
        "tokens": scatter_about(streams_of[0], (TOKENS, D), 1.0, 6.0, ((0, 128),)),
        "modality": draw_modality(jax.random.fold_in(streams_of[9], 71), 0),
        "norm_gain": jnp.clip(1.0 + 0.18 * jax.random.normal(streams_of[2], (2, D), jnp.float32), 0.1, 1.9),
        "picks": draw_picks(jax.random.fold_in(streams_of[9], 71), 0),
        "counts": draw_counts(jax.random.fold_in(streams_of[9], 71), 0),
        "router": scatter_about(streams_of[5], (EXPERTS, D), D ** -0.5, 0.0625, ((0, 8),)),
        "gate_weight": scatter_about(streams_of[6], (EXPERTS, D, FFW), D ** -0.5, 0.0625, ((0, 8), (2, 16))),
        "up_weight": scatter_about(streams_of[7], (EXPERTS, D, FFW), D ** -0.5, 0.0625, ((0, 8), (2, 16))),
        "down_weight": scatter_about(streams_of[8], (EXPERTS, FFW, D), FFW ** -0.5, 0.09375, ((0, 8), (1, 16))),
    }


EPSILON = 1e-05

def reference(tokens, modality, norm_gain, picks, counts, router, gate_weight, up_weight, down_weight):
    values = tokens.astype(jnp.float32)
    square = lax.optimization_barrier(jnp.mean(values * values, axis=1, keepdims=True))
    gain_rows = jnp.where(modality[:, None] == 1, norm_gain[1][None, :], norm_gain[0][None, :]).astype(jnp.float32)
    normed = (values * lax.rsqrt(square + EPSILON) * gain_rows).astype(jnp.bfloat16)
    block_width = FFW // N_DP

    def one_expert(combined, expert_index):
        selected = picks[expert_index].reshape(-1).astype(jnp.int32)
        chosen = jnp.take(normed, selected, axis=0)
        gate_value = jnp.dot(chosen, gate_weight[expert_index], preferred_element_type=jnp.float32)
        up_value = jnp.dot(chosen, up_weight[expert_index], preferred_element_type=jnp.float32)
        hidden = (jax.nn.silu(gate_value) * up_value).astype(jnp.bfloat16)
        weight = jax.nn.sigmoid(jnp.dot(chosen, router[expert_index], preferred_element_type=jnp.float32))
        accumulate = jnp.zeros((chosen.shape[0], D), jnp.float32)
        for block_index in range(N_DP):
            low = block_index * block_width
            hidden_part = jnp.dot(hidden[:, low:low + block_width], down_weight[expert_index, low:low + block_width, :], preferred_element_type=jnp.float32)
            rounded = lax.optimization_barrier((weight[:, None] * hidden_part).astype(jnp.bfloat16))
            accumulate = accumulate + rounded.astype(jnp.float32)
        expert_out = accumulate.astype(jnp.bfloat16)
        usable = (jnp.arange(PICK)[None, :] < counts[expert_index][:, None]).reshape(-1)
        added = jnp.where(usable[:, None], expert_out.astype(jnp.float32), jnp.float32(0.0))
        return (combined.at[selected].add(added), None)
    combined, _ = lax.scan(one_expert, jnp.zeros((TOKENS, D), jnp.float32), jnp.arange(EXPERTS))
    return (values + combined).astype(jnp.bfloat16)
```

```python
import jax
import jax.numpy as jnp
from jax import lax
from jax.sharding import PartitionSpec as P

EPSILON = 1e-05


def expert_block(chosen, router, gate_weight, up_weight, down_weight):
    piece = lax.all_gather(chosen, "dp", axis=0, tiled=True)
    gate_value = jnp.dot(piece, gate_weight[0], preferred_element_type=jnp.float32)
    up_value = jnp.dot(piece, up_weight[0], preferred_element_type=jnp.float32)
    hidden_hidden = (jax.nn.silu(gate_value) * up_value).astype(jnp.bfloat16)
    router_score = jnp.dot(piece, router[0], preferred_element_type=jnp.float32)
    weight = jax.nn.sigmoid(router_score)
    return lax.psum_scatter(
        (
            weight[:, None]
            * jnp.dot(hidden_hidden, down_weight[0], preferred_element_type=jnp.float32)
        ).astype(jnp.bfloat16),
        "dp",
        scatter_dimension=0,
        tiled=True,
    )


def shards(tokens, modality, norm_gain, picks, counts, router, gate_weight, up_weight, down_weight):
    tok_rows = tokens.shape[0]
    groups = lax.axis_size("expert")
    pick_slots = picks.shape[2]
    flat_index = lax.axis_index(("dp", "expert"))
    values = tokens.astype(jnp.float32)
    square = jnp.mean(values * values, axis=1, keepdims=True)
    gain_rows = jnp.where(modality[:, None] == 1, norm_gain[1][None, :], norm_gain[0][None, :])
    normed = (values * lax.rsqrt(square + EPSILON) * gain_rows).astype(jnp.bfloat16)
    local_rows = picks[:, 0, :] - flat_index * tok_rows
    outgoing = jnp.take(normed, local_rows.reshape(-1), axis=0).reshape(groups, pick_slots, -1)
    incoming = lax.all_to_all(outgoing, "expert", split_axis=0, concat_axis=0, tiled=True)
    slots = incoming.reshape(groups * pick_slots, -1)
    expert = lax.axis_index("expert")
    group_counts = lax.dynamic_slice(counts, (expert, lax.axis_index("dp") * groups), (1, groups))[0]
    live = (jnp.arange(pick_slots)[None, :] < group_counts[:, None]).reshape(-1)
    place = jnp.cumsum(live.astype(jnp.int32)) - 1
    live_rows = groups * pick_slots // 2
    packing = ((jnp.arange(live_rows)[:, None] == place[None, :]) & live[None, :]).astype(jnp.bfloat16)
    chosen = jnp.dot(packing, slots, preferred_element_type=jnp.float32).astype(jnp.bfloat16)
    answers = expert_block(chosen, router, gate_weight, up_weight, down_weight)
    answers = jnp.dot(packing.T, answers, preferred_element_type=jnp.float32).astype(jnp.bfloat16)
    returned = lax.all_to_all(
        answers.reshape(groups, pick_slots, -1), "expert", split_axis=0, concat_axis=0, tiled=True
    )
    own_counts = lax.dynamic_index_in_dim(counts, flat_index, 1, keepdims=False)
    usable = (jnp.arange(pick_slots)[None, :] < own_counts[:, None]).reshape(-1)
    placing = (
        (local_rows.reshape(-1)[None, :] == jnp.arange(tok_rows)[:, None]) & usable[None, :]
    ).astype(jnp.bfloat16)
    combined = jnp.dot(
        placing, returned.reshape(groups * pick_slots, -1), preferred_element_type=jnp.float32
    )
    return (values + combined).astype(jnp.bfloat16)


def solution(mesh):
    placed = (
        P(("dp", "expert"), None),
        P(("dp", "expert")),
        P(),
        P(None, ("dp", "expert"), None),
        P(),
        P("expert", None),
        P("expert", None, "dp"),
        P("expert", None, "dp"),
        P("expert", "dp", None),
    )
    return jax.shard_map(
        shards, mesh=mesh, in_specs=placed, out_specs=P(("dp", "expert"), None), check_vma=False
    )
```

```python
import functools

import jax
import jax.numpy as jnp
from jax import lax
from jax.experimental import pallas as pl
from jax.experimental.pallas import tpu as pltpu
from jax.sharding import PartitionSpec as P

EPSILON = 1e-05
MESH = pl.DeviceIdType.MESH
SIDE = 4
GROUP = 8
CHUNKS = 4
F32 = jnp.float32
BF16 = jnp.bfloat16


def iota(shape, dim):
    return lax.broadcasted_iota(jnp.int32, shape, dim)


def kernel(
    tokens, gain, picks, counts, router, gate, up, down, out,
    tok, w1, w2, so, sr, x, acc, hid, part, r1, f1, red, r2, f2, ro, rr, ob, score, mats,
    local_sem, a2a_send, a2a_recv, ag_send, ag_p1, ag_p2, rs_send, rs_p1, rs_p2, ret_send, ret_recv, out_sem,
):
    dp, e = lax.axis_index("dp"), lax.axis_index("expert")
    y, z = dp // SIDE, dp % SIDE
    half = tokens.shape[1] // 2
    cols = half // CHUNKS
    ntok = tokens.shape[0]
    rows = x.shape[2] // (SIDE * SIDE)
    hr = rows // 2
    live_cap = rows

    def near(h, axis, step):
        along_y = (h == 0) == (axis == "a")
        if along_y:
            return (lax.rem(y + step + SIDE, SIDE) * SIDE + z, e)
        return (y * SIDE + lax.rem(z + step + SIDE, SIDE), e)

    def other(o):
        return (dp, lax.rem(e + o, GROUP))

    def send(src, dst, ssem, rsem, device):
        pltpu.make_async_remote_copy(
            src_ref=src, dst_ref=dst, send_sem=ssem, recv_sem=rsem, device_id=device, device_id_type=MESH
        ).start()

    def settle(ref, sem):
        pltpu.make_async_copy(ref, ref, sem).wait()

    barrier = pltpu.get_barrier_semaphore()
    for step in (-1, 1):
        for axis in "ab":
            pl.semaphore_signal(barrier, 1, device_id=near(0, axis, step), device_id_type=MESH)
    for o in range(1, GROUP):
        pl.semaphore_signal(barrier, 1, device_id=other(o), device_id_type=MESH)

    loads = []
    for h in range(2):
        cp = pltpu.make_async_copy(tokens.at[:, pl.ds(h * half, half)], tok.at[h], local_sem.at[h])
        cp.start()
        loads.append(cp)
    big = [
        pltpu.make_async_copy(gate.at[0], w1.at[:, pl.ds(0, gate.shape[2])], local_sem.at[2]),
        pltpu.make_async_copy(up.at[0], w1.at[:, pl.ds(gate.shape[2], gate.shape[2])], local_sem.at[3]),
        pltpu.make_async_copy(down.at[0], w2, local_sem.at[4]),
    ]

    nslot = GROUP * 16
    lane = iota((8, nslot), 1)
    lane_e, lane_h, lane_k = lane >> 4, (lane >> 3) & 1, lane & 7
    sub = iota((8, nslot), 0)
    pk = picks[:, 0, :] - (dp * GROUP + e) * ntok
    spread = jnp.zeros((8, nslot), jnp.int32)
    for k in range(8):
        spread = spread + jnp.where(lane_k == k, pk[:, k : k + 1], 0)
    pick_row = jnp.sum(jnp.where(sub == lane_e, spread, 0).astype(F32), axis=0, keepdims=True)
    cnt = jnp.sum(jnp.where(sub == e, counts[...], 0).astype(F32), axis=0, keepdims=True)
    cnt16 = jnp.broadcast_to(cnt, (16, nslot)).astype(BF16)
    src = iota((nslot, nslot), 0) - dp * GROUP
    dst_e = iota((nslot, nslot), 1) >> 4
    same = (src == dst_e).astype(F32).astype(BF16)
    before = ((src >= 0) & (src < dst_e)).astype(F32).astype(BF16)
    cnt_r = jnp.dot(cnt16, same, preferred_element_type=F32)[0:1]
    off_r = jnp.dot(cnt16, before, preferred_element_type=F32)[0:1]
    k_r = lane_k[0:1].astype(F32)
    pos_r = jnp.where(k_r < cnt_r, off_r + k_r, -1.0)

    def placing(n, shift):
        q = iota((2 * n, nslot), 0)
        l = iota((2 * n, nslot), 1)
        return ((q >> shift) == ((l >> 3) & 1)), (q & (n - 1)).astype(F32)

    same_half, t_id = placing(ntok, 7)
    put = jnp.where(same_half & (t_id == pick_row), 1.0, 0.0)
    same_half, p_id = placing(live_cap, 5)
    pack = jnp.where(same_half & (p_id == pos_r), 1.0, 0.0)
    take_m = put.T.astype(BF16)
    mats[0 : 2 * ntok, :] = put.astype(BF16)
    mats[2 * ntok : 2 * ntok + 2 * live_cap, :] = pack.astype(BF16)
    unpack_m = pack.T.astype(BF16)

    for cp in loads:
        cp.wait()
    for cp in big:
        cp.start()
    total = jnp.zeros((nslot, 128), F32)
    for k in range(CHUNKS):
        t = tok[:, :, pl.ds(k * cols, cols)].reshape(2 * ntok, cols)
        g = jnp.dot(take_m, t, preferred_element_type=F32)
        so[k] = g.astype(BF16).reshape(GROUP, 16, cols)
        sq = g * g
        for i in range(cols // 128):
            total = total + sq[:, i * 128 : (i + 1) * 128]
    ss = jnp.broadcast_to(jnp.sum(total, axis=1, keepdims=True), (nslot, 128))
    h_col = (iota((nslot, 128), 0) >> 3) & 1
    pair = jnp.where(h_col == 0, pltpu.roll(ss, nslot - 8, 0), pltpu.roll(ss, 8, 0))
    inv = lax.rsqrt((ss + pair)[:, 0:1] / (2 * half) + EPSILON)
    first = h_col[:, 0:1] == 0
    text = iota((nslot, 1), 0) < nslot // 2

    for k in range(CHUNKS):
        ga = gain[:, pl.ds(k * cols, cols)]
        gb = gain[:, pl.ds(half + k * cols, cols)]
        gm = jnp.where(
            first,
            jnp.where(text, ga[0:1], ga[1:2]),
            jnp.where(text, gb[0:1], gb[1:2]),
        )
        g = so[k].reshape(nslot, cols).astype(F32)
        so[k] = (g * inv * gm).astype(BF16).reshape(GROUP, 16, cols)
        if k == 0:
            pl.semaphore_wait(barrier, 4 + GROUP - 1)
        for o in (4, 3, 5, 2, 6, 7, 1):
            to = lax.rem(e + o, GROUP)
            send(so.at[k, to], sr.at[k, e], a2a_send.at[k], a2a_recv.at[k], other(o))
        sr[k, e] = so[k, e]

    score[...] = jnp.zeros_like(score)
    acc[...] = jnp.zeros_like(acc)

    def place(h, da, db):
        dy, dz = (da, db) if h == 0 else (db, da)
        return (dy * SIDE + dz) * rows

    def blk(h, k, da, db, part_=None):
        base = place(h, da, db)
        if part_ is None:
            return x.at[h, k, pl.ds(base, rows)]
        return x.at[h, k, pl.ds(base + part_ * hr, hr)]

    def second(h, k, da):
        s = ag_send.at[h, k]
        send(blk(h, k, da, 0), blk(h, k, da, 1), s, ag_p2.at[h, k, da, 0], near(h, "b", 1))
        send(blk(h, k, da, 0), blk(h, k, da, 3), s, ag_p2.at[h, k, da, 1], near(h, "b", -1))

    def stage_a(k):
        settle(sr.at[k, pl.ds(0, GROUP - 1)], a2a_recv.at[k])
        packed = jnp.dot(
            mats[2 * ntok : 2 * ntok + 2 * live_cap, :], sr[k].reshape(nslot, cols), preferred_element_type=F32
        )
        both = packed.astype(BF16)
        x[0, k, 0:rows] = both[0:rows]
        x[1, k, 0:rows] = both[rows : 2 * rows]
        for h in range(2):
            s = ag_send.at[h, k]
            send(blk(h, k, 0, 0), blk(h, k, 1, 0), s, ag_p1.at[h, k, 0], near(h, "a", 1))
            send(blk(h, k, 0, 0), blk(h, k, 3, 0), s, ag_p1.at[h, k, 1], near(h, "a", -1))
        for h in range(2):
            second(h, k, 0)
        prod = packed[0:rows] * router[:, pl.ds(k * cols, cols)].astype(F32)
        prod += packed[rows : 2 * rows] * router[:, pl.ds(half + k * cols, cols)].astype(F32)
        s = score[...]
        for i in range(cols // 128):
            s = s + prod[:, i * 128 : (i + 1) * 128]
        score[...] = s

    def stage_b(k):
        for h in range(2):
            s = ag_send.at[h, k]
            settle(blk(h, k, 1, 0), ag_p1.at[h, k, 0])
            send(blk(h, k, 1, 0, 0), blk(h, k, 2, 0, 0), s, ag_p1.at[h, k, 2], near(h, "a", 1))
            settle(blk(h, k, 3, 0), ag_p1.at[h, k, 1])
            send(blk(h, k, 3, 0, 1), blk(h, k, 2, 0, 1), s, ag_p1.at[h, k, 3], near(h, "a", -1))
        for h in range(2):
            second(h, k, 1)
            second(h, k, 3)

    def stage_c(k):
        for h in range(2):
            settle(blk(h, k, 2, 0, 0), ag_p1.at[h, k, 2])
            settle(blk(h, k, 2, 0, 1), ag_p1.at[h, k, 3])
            second(h, k, 2)

    def stage_d(k, das):
        for da in das:
            for h in range(2):
                s = ag_send.at[h, k]
                settle(blk(h, k, da, 1), ag_p2.at[h, k, da, 0])
                send(blk(h, k, da, 1, 0), blk(h, k, da, 2, 0), s, ag_p2.at[h, k, da, 2], near(h, "b", 1))
                settle(blk(h, k, da, 3), ag_p2.at[h, k, da, 1])
                send(blk(h, k, da, 3, 1), blk(h, k, da, 2, 1), s, ag_p2.at[h, k, da, 3], near(h, "b", -1))

    def stage_e(k):
        if k == 0:
            big[0].wait()
            big[1].wait()
        for h in range(2):
            for da in range(SIDE):
                settle(blk(h, k, da, 2, 0), ag_p2.at[h, k, da, 2])
                settle(blk(h, k, da, 2, 1), ag_p2.at[h, k, da, 3])
        for h in range(2):
            acc[...] += jnp.dot(x[h, k], w1[pl.ds(h * half + k * cols, cols), :], preferred_element_type=F32)

    stage_a(0)
    for k in range(CHUNKS):
        stage_b(k)
        stage_d(k, (0,))
        if k + 1 < CHUNKS:
            stage_a(k + 1)
        stage_c(k)
        stage_d(k, (1, 3))
        if k > 0:
            stage_e(k - 1)
        stage_d(k, (2,))
    stage_e(CHUNKS - 1)

    width = acc.shape[1] // 2
    gv, uv = acc[:, 0:width], acc[:, width : 2 * width]
    hid[...] = (gv / (1.0 + jnp.exp(-gv)) * uv).astype(BF16)
    weight = jax.nn.sigmoid(jnp.sum(score[...], axis=1, keepdims=True))
    big[2].wait()

    def multiply(k):
        for h in range(2):
            for t in range(0, cols, 256):
                w = w2[:, pl.ds(h * half + k * cols + t, 256)]
                v = jnp.dot(hid[...], w, preferred_element_type=F32).astype(BF16)
                for da in range(SIDE):
                    for db in range(SIDE):
                        base = place(h, da, db)
                        for q in range(2):
                            part[h, k, db, q, da * hr : (da + 1) * hr, t : t + 256] = v[
                                base + q * hr : base + (q + 1) * hr
                            ]
            s = rs_send.at[h, k, 0]
            send(part.at[h, k, 2, 0], r1.at[h, k, 0], s, rs_p1.at[h, k, 0], near(h, "b", -1))
            send(part.at[h, k, 2, 1], r1.at[h, k, 1], s, rs_p1.at[h, k, 1], near(h, "b", 1))
            send(part.at[h, k, 1, 1], f1.at[h, k, 0, 1], s, rs_p1.at[h, k, 2], near(h, "b", -1))
            send(part.at[h, k, 3, 0], f1.at[h, k, 1, 0], s, rs_p1.at[h, k, 3], near(h, "b", 1))

    def first_on(k):
        for h in range(2):
            s = rs_send.at[h, k, 0]
            settle(r1.at[h, k, 0], rs_p1.at[h, k, 0])
            part[h, k, 1, 0] = (part[h, k, 1, 0].astype(F32) + r1[h, k, 0].astype(F32)).astype(BF16)
            send(part.at[h, k, 1, 0], f1.at[h, k, 0, 0], s, rs_p1.at[h, k, 4], near(h, "b", -1))
            settle(r1.at[h, k, 1], rs_p1.at[h, k, 1])
            part[h, k, 3, 1] = (part[h, k, 3, 1].astype(F32) + r1[h, k, 1].astype(F32)).astype(BF16)
            send(part.at[h, k, 3, 1], f1.at[h, k, 1, 1], s, rs_p1.at[h, k, 5], near(h, "b", 1))

    def first_end(k):
        for h in range(2):
            settle(f1.at[h, k, 0, 1], rs_p1.at[h, k, 2])
            settle(f1.at[h, k, 1, 0], rs_p1.at[h, k, 3])
            settle(f1.at[h, k, 0, 0], rs_p1.at[h, k, 4])
            settle(f1.at[h, k, 1, 1], rs_p1.at[h, k, 5])
            for q in range(2):
                v = part[h, k, 0, q].astype(F32) + f1[h, k, 0, q].astype(F32) + f1[h, k, 1, q].astype(F32)
                v = v.astype(BF16)
                for da in range(SIDE):
                    red[h, k, da, q] = v[da * hr : (da + 1) * hr]
            s = rs_send.at[h, k, 1]
            send(red.at[h, k, 2, 0], r2.at[h, k, 0], s, rs_p2.at[h, k, 0], near(h, "a", -1))
            send(red.at[h, k, 2, 1], r2.at[h, k, 1], s, rs_p2.at[h, k, 1], near(h, "a", 1))
            send(red.at[h, k, 1, 1], f2.at[h, k, 0, 1], s, rs_p2.at[h, k, 2], near(h, "a", -1))
            send(red.at[h, k, 3, 0], f2.at[h, k, 1, 0], s, rs_p2.at[h, k, 3], near(h, "a", 1))

    def second_on(k):
        for h in range(2):
            s = rs_send.at[h, k, 1]
            settle(r2.at[h, k, 0], rs_p2.at[h, k, 0])
            red[h, k, 1, 0] = (red[h, k, 1, 0].astype(F32) + r2[h, k, 0].astype(F32)).astype(BF16)
            send(red.at[h, k, 1, 0], f2.at[h, k, 0, 0], s, rs_p2.at[h, k, 4], near(h, "a", -1))
            settle(r2.at[h, k, 1], rs_p2.at[h, k, 1])
            red[h, k, 3, 1] = (red[h, k, 3, 1].astype(F32) + r2[h, k, 1].astype(F32)).astype(BF16)
            send(red.at[h, k, 3, 1], f2.at[h, k, 1, 1], s, rs_p2.at[h, k, 5], near(h, "a", 1))

    def second_end(k):
        res = []
        for h in range(2):
            settle(f2.at[h, k, 0, 1], rs_p2.at[h, k, 2])
            settle(f2.at[h, k, 1, 0], rs_p2.at[h, k, 3])
            settle(f2.at[h, k, 0, 0], rs_p2.at[h, k, 4])
            settle(f2.at[h, k, 1, 1], rs_p2.at[h, k, 5])
            v = red[h, k, 0].astype(F32) + f2[h, k, 0].astype(F32) + f2[h, k, 1].astype(F32)
            res.append((v.reshape(rows, cols) * weight).astype(BF16))
        res = jnp.concatenate(res, axis=0)
        back = jnp.dot(unpack_m, res, preferred_element_type=F32)
        ro[k] = back.astype(BF16).reshape(GROUP, 16, cols)
        for o in (4, 3, 5, 2, 6, 7, 1):
            to = lax.rem(e + o, GROUP)
            send(ro.at[k, to], rr.at[k, e], ret_send.at[k], ret_recv.at[k], other(o))
        rr[k, e] = ro[k, e]

    def finish(k):
        settle(rr.at[k, pl.ds(0, GROUP - 1)], ret_recv.at[k])
        v = jnp.dot(mats[0 : 2 * ntok, :], rr[k].reshape(nslot, cols), preferred_element_type=F32)
        t = tok[:, :, pl.ds(k * cols, cols)].reshape(2 * ntok, cols).astype(F32)
        ob[k] = (t + v).astype(BF16).reshape(2, ntok, cols)
        for h in range(2):
            pltpu.make_async_copy(
                ob.at[k, h], out.at[:, pl.ds(h * half + k * cols, cols)], out_sem.at[h, k]
            ).start()

    multiply(0)
    for k in range(CHUNKS + 2):
        if k < CHUNKS:
            if k + 1 < CHUNKS:
                multiply(k + 1)
            first_on(k)
        if 0 <= k - 1 < CHUNKS:
            second_on(k - 1)
        if k < CHUNKS:
            first_end(k)
        if 0 <= k - 1 < CHUNKS:
            second_end(k - 1)
        if 0 <= k - 2 < CHUNKS:
            finish(k - 2)

    for k in range(CHUNKS):
        for h in range(2):
            settle(x.at[h, k, pl.ds(0, 15 * rows)], ag_send.at[h, k])
            settle(part.at[h, k, pl.ds(0, 3)], rs_send.at[h, k, 0])
            settle(red.at[h, k, pl.ds(0, 3)], rs_send.at[h, k, 1])
            pltpu.make_async_copy(
                ob.at[k, h], out.at[:, pl.ds(h * half + k * cols, cols)], out_sem.at[h, k]
            ).wait()
        settle(so.at[k, pl.ds(0, GROUP - 1)], a2a_send.at[k])
        settle(ro.at[k, pl.ds(0, GROUP - 1)], ret_send.at[k])


def shards(tokens, modality, norm_gain, picks, counts, router, gate_weight, up_weight, down_weight):
    ntok, d = tokens.shape
    half = d // 2
    cols = half // CHUNKS
    hidden = gate_weight.shape[2]
    rows = GROUP * picks.shape[2] // 2
    hr = rows // 2
    places = SIDE * SIDE
    vmem = pl.BlockSpec(memory_space=pltpu.VMEM)
    anywhere = pl.BlockSpec(memory_space=pl.ANY)
    dma = pltpu.SemaphoreType.DMA
    slots = rows * places
    flops = 2 * slots * d * hidden * 3
    return pl.pallas_call(
        kernel,
        name="expert_layer",
        out_shape=jax.ShapeDtypeStruct((ntok, d), BF16),
        in_specs=[anywhere, vmem, vmem, vmem, vmem, anywhere, anywhere, anywhere],
        out_specs=anywhere,
        scratch_shapes=[
            pltpu.VMEM((2, ntok, half), BF16),
            pltpu.VMEM((d, 2 * hidden), BF16),
            pltpu.VMEM((hidden, d), BF16),
            pltpu.VMEM((CHUNKS, GROUP, 16, cols), BF16),
            pltpu.VMEM((CHUNKS, GROUP, 16, cols), BF16),
            pltpu.VMEM((2, CHUNKS, slots, cols), BF16),
            pltpu.VMEM((slots, 2 * hidden), F32),
            pltpu.VMEM((slots, hidden), BF16),
            pltpu.VMEM((2, CHUNKS, SIDE, 2, SIDE * hr, cols), BF16),
            pltpu.VMEM((2, CHUNKS, 2, SIDE * hr, cols), BF16),
            pltpu.VMEM((2, CHUNKS, 2, 2, SIDE * hr, cols), BF16),
            pltpu.VMEM((2, CHUNKS, SIDE, 2, hr, cols), BF16),
            pltpu.VMEM((2, CHUNKS, 2, hr, cols), BF16),
            pltpu.VMEM((2, CHUNKS, 2, 2, hr, cols), BF16),
            pltpu.VMEM((CHUNKS, GROUP, 16, cols), BF16),
            pltpu.VMEM((CHUNKS, GROUP, 16, cols), BF16),
            pltpu.VMEM((CHUNKS, 2, ntok, cols), BF16),
            pltpu.VMEM((rows, 128), F32),
            pltpu.VMEM((2 * ntok + 2 * rows, GROUP * 16), BF16),
            dma((5,)),
            dma((CHUNKS,)),
            dma((CHUNKS,)),
            dma((2, CHUNKS)),
            dma((2, CHUNKS, 4)),
            dma((2, CHUNKS, SIDE, 4)),
            dma((2, CHUNKS, 2)),
            dma((2, CHUNKS, 6)),
            dma((2, CHUNKS, 6)),
            dma((CHUNKS,)),
            dma((CHUNKS,)),
            dma((2, CHUNKS)),
        ],
        compiler_params=pltpu.CompilerParams(
            collective_id=0, has_side_effects=True, vmem_limit_bytes=60 * 2**20
        ),
        cost_estimate=pl.CostEstimate(flops=flops, bytes_accessed=16 * 2**20, transcendentals=slots * hidden),
    )(tokens, norm_gain, picks, counts, router, gate_weight, up_weight, down_weight)


def solution(mesh):
    placed = (
        P(("dp", "expert"), None),
        P(("dp", "expert")),
        P(),
        P(None, ("dp", "expert"), None),
        P(),
        P("expert", None),
        P("expert", None, "dp"),
        P("expert", None, "dp"),
        P("expert", "dp", None),
    )
    return jax.shard_map(
        shards, mesh=mesh, in_specs=placed, out_specs=P(("dp", "expert"), None), check_vma=False
    )
```

```python
import functools

import jax
import jax.numpy as jnp
from jax import lax
from jax.experimental import pallas as pl
from jax.experimental.pallas import tpu as pltpu
from jax.sharding import PartitionSpec as P

EPSILON = 1e-05
MESH = pl.DeviceIdType.MESH
SIDE = 4
GROUP = 8
F32 = jnp.float32
BF16 = jnp.bfloat16
NEAR = pl.ds(1, 2)
EXCHANGES = ((0, 512), (512, 512), (1024, 1024), (2048, 2048))
GATHERS = ((0, 0, 512), (0, 512, 512), (0, 1024, 1024), (0, 2048, 2048), (1, 0, 1024), (1, 1024, 1024), (1, 2048, 1024), (1, 3072, 1024))
REDUCES = ((0, 0, 1024), (0, 1024, 1024), (0, 2048, 1024), (0, 3072, 1024), (1, 0, 1024), (1, 1024, 1024), (1, 2048, 1024), (1, 3072, 1024))
RETURNS = ((0, 1024), (1024, 1024), (2048, 1024), (3072, 1024))


def iota(shape, dim):
    return lax.broadcasted_iota(jnp.int32, shape, dim)


def kernel(
    tokens, gain, picks, counts, router, gate, up, down, out,
    tok, w1, w2, so, sr, x, acc, hid, part, r1, f1, red, r2, f2, res, ro, rr, ob, score, mats,
    local_sem, a2a_send, a2a_recv, ag_send, ag_p1, ag_p2, rs_send, rs_p1, rs_p2, ret_send, ret_recv, out_sem,
):
    dp, e = lax.axis_index("dp"), lax.axis_index("expert")
    y, z = dp // SIDE, dp % SIDE
    half = tokens.shape[1] // 2
    ntok = tokens.shape[0]
    hr = x.shape[4]
    rows = 2 * hr
    slots = SIDE * SIDE * hr
    width = gate.shape[2]

    def near(h, axis, step):
        along_y = (h == 0) == (axis == "a")
        if along_y:
            return (lax.rem(y + step + SIDE, SIDE) * SIDE + z, e)
        return (y * SIDE + lax.rem(z + step + SIDE, SIDE), e)

    def other(o):
        return (dp, lax.rem(e + o, GROUP))

    def send(src, dst, ssem, rsem, device):
        pltpu.make_async_remote_copy(
            src_ref=src, dst_ref=dst, send_sem=ssem, recv_sem=rsem, device_id=device, device_id_type=MESH
        ).start()

    def settle(ref, sem):
        pltpu.make_async_copy(ref, ref, sem).wait()

    barrier = pltpu.get_barrier_semaphore()
    for step in (-1, 1):
        for axis in "ab":
            pl.semaphore_signal(barrier, 1, device_id=near(0, axis, step), device_id_type=MESH)
    for o in range(1, GROUP):
        pl.semaphore_signal(barrier, 1, device_id=other(o), device_id_type=MESH)

    loads = []
    for h in range(2):
        cp = pltpu.make_async_copy(tokens.at[:, pl.ds(h * half, half)], tok.at[h], local_sem.at[h])
        cp.start()
        loads.append(cp)
    big = [
        pltpu.make_async_copy(gate.at[0], w1.at[:, pl.ds(0, width)], local_sem.at[2]),
        pltpu.make_async_copy(up.at[0], w1.at[:, pl.ds(width, width)], local_sem.at[3]),
        pltpu.make_async_copy(down.at[0], w2, local_sem.at[4]),
    ]

    nslot = GROUP * 16
    lane = iota((8, nslot), 1)
    lane_e, lane_h, lane_k = lane >> 4, (lane >> 3) & 1, lane & 7
    sub = iota((8, nslot), 0)
    pk = picks[:, 0, :] - (dp * GROUP + e) * ntok
    spread = jnp.zeros((8, nslot), jnp.int32)
    for k in range(8):
        spread = spread + jnp.where(lane_k == k, pk[:, k : k + 1], 0)
    pick_row = jnp.sum(jnp.where(sub == lane_e, spread, 0).astype(F32), axis=0, keepdims=True)
    cnt = jnp.sum(jnp.where(sub == e, counts[...], 0).astype(F32), axis=0, keepdims=True)
    cnt16 = jnp.broadcast_to(cnt, (16, nslot)).astype(BF16)
    src = iota((nslot, nslot), 0) - dp * GROUP
    dst_e = iota((nslot, nslot), 1) >> 4
    same = (src == dst_e).astype(F32).astype(BF16)
    before = ((src >= 0) & (src < dst_e)).astype(F32).astype(BF16)
    cnt_r = jnp.dot(cnt16, same, preferred_element_type=F32)[0:1]
    off_r = jnp.dot(cnt16, before, preferred_element_type=F32)[0:1]
    k_r = lane_k[0:1].astype(F32)
    pos_r = jnp.where(k_r < cnt_r, off_r + k_r, -1.0)

    def placing(n, shift):
        q = iota((2 * n, nslot), 0)
        l = iota((2 * n, nslot), 1)
        return ((q >> shift) == ((l >> 3) & 1)), (q & (n - 1)).astype(F32)

    same_half, t_id = placing(ntok, 7)
    put = jnp.where(same_half & (t_id == pick_row), 1.0, 0.0)
    same_half, p_id = placing(rows, 5)
    pack = jnp.where(same_half & (p_id == pos_r), 1.0, 0.0)
    take_m = put.T.astype(BF16)
    mats[0 : 2 * ntok, :] = put.astype(BF16)
    mats[2 * ntok : 2 * ntok + 2 * rows, :] = pack.astype(BF16)
    unpack_m = pack.T.astype(BF16)

    for cp in loads:
        cp.wait()
    total = jnp.zeros((nslot, 128), F32)
    for c in range(0, half, 1024):
        t = tok[:, :, pl.ds(c, 1024)].reshape(2 * ntok, 1024)
        g = jnp.dot(take_m, t, preferred_element_type=F32)
        so[:, :, pl.ds(c, 1024)] = g.astype(BF16).reshape(GROUP, 16, 1024)
        sq = g * g
        for i in range(1024 // 128):
            total = total + sq[:, i * 128 : (i + 1) * 128]
    ss = jnp.broadcast_to(jnp.sum(total, axis=1, keepdims=True), (nslot, 128))
    h_col = (iota((nslot, 128), 0) >> 3) & 1
    pair = jnp.where(h_col == 0, pltpu.roll(ss, nslot - 8, 0), pltpu.roll(ss, 8, 0))
    inv = lax.rsqrt((ss + pair)[:, 0:1] / (2 * half) + EPSILON)
    first = h_col[:, 0:1] == 0
    text = iota((nslot, 1), 0) < nslot // 2

    def norm(i):
        c, w = EXCHANGES[i]
        at = pl.ds(c, w)
        ga = gain[:, at]
        gb = gain[:, pl.ds(half + c, w)]
        gm = jnp.where(
            first,
            jnp.where(text, ga[0:1], ga[1:2]),
            jnp.where(text, gb[0:1], gb[1:2]),
        )
        g = so[:, :, at].reshape(nslot, w).astype(F32)
        so[:, :, at] = (g * inv * gm).astype(BF16).reshape(GROUP, 16, w)
        if i == 0:
            pl.semaphore_wait(barrier, 4 + GROUP - 1)
        for o in (4, 3, 5, 2, 6, 7, 1):
            to = lax.rem(e + o, GROUP)
            send(so.at[to, :, at], sr.at[e, :, at], a2a_send.at[i], a2a_recv.at[i], other(o))
        sr[e, :, at] = so[e, :, at]

    def load_weights():
        for cp in big:
            cp.start()

    def clear():
        score[...] = jnp.zeros_like(score)

    def packing(i):
        c, w = EXCHANGES[i]
        at = pl.ds(c, w)
        settle(sr.at[pl.ds(0, GROUP - 1), :, at], a2a_recv.at[i])
        packed = jnp.dot(
            mats[2 * ntok : 2 * ntok + 2 * rows, :], sr[:, :, at].reshape(nslot, w), preferred_element_type=F32
        )
        both = packed.astype(BF16)
        for h in range(2):
            for g in range(2):
                x[h, g, 0, 0, :, at] = both[h * rows + g * hr : h * rows + (g + 1) * hr]
        prod = packed[0:rows] * router[:, at].astype(F32)
        prod += packed[rows : 2 * rows] * router[:, pl.ds(half + c, w)].astype(F32)
        s = score[...]
        for t in range(w // 128):
            s = s + prod[:, t * 128 : (t + 1) * 128]
        score[...] = s

    def blk(h, g, da, db, c, w):
        if h == 1:
            da, db = db, da
        return x.at[h, g, da, db, :, pl.ds(c, w)]

    SETS = (0, NEAR, 3)

    def second(i, n):
        g, c, w = GATHERS[i]
        da = SETS[n]
        for h in range(2):
            s = ag_send.at[h, i, 1]
            send(blk(h, g, da, 0, c, w), blk(h, g, da, 1, c, w), s, ag_p2.at[h, i, n, 0], near(h, "b", 1))
            send(blk(h, g, da, 0, c, w), blk(h, g, da, 2, c, w), s, ag_p2.at[h, i, n, 1], near(h, "b", -1))

    def own(i):
        g, c, w = GATHERS[i]
        for h in range(2):
            s = ag_send.at[h, i, 0]
            send(blk(h, g, 0, 0, c, w), blk(h, g, 1, 0, c, w), s, ag_p1.at[h, i, 0], near(h, "a", 1))
            send(blk(h, g, 0, 0, c, w), blk(h, g, 2, 0, c, w), s, ag_p1.at[h, i, 1], near(h, "a", -1))

    def own2(i):
        second(i, 0)

    def first_hop(i):
        g, c, w = GATHERS[i]
        hw = w // 2
        for h in range(2):
            s = ag_send.at[h, i, 0]
            settle(blk(h, g, 1, 0, c, w), ag_p1.at[h, i, 0])
            send(blk(h, g, 1, 0, c, hw), blk(h, g, 3, 0, c, hw), s, ag_p1.at[h, i, 2], near(h, "a", 1))
            settle(blk(h, g, 2, 0, c, w), ag_p1.at[h, i, 1])
            send(blk(h, g, 2, 0, c + hw, hw), blk(h, g, 3, 0, c + hw, hw), s, ag_p1.at[h, i, 3], near(h, "a", -1))
        second(i, 1)

    def second_hop(i):
        g, c, w = GATHERS[i]
        hw = w // 2
        for h in range(2):
            settle(blk(h, g, 3, 0, c, hw), ag_p1.at[h, i, 2])
            settle(blk(h, g, 3, 0, c + hw, hw), ag_p1.at[h, i, 3])
        second(i, 2)

    def forward(i, n):
        g, c, w = GATHERS[i]
        hw = w // 2
        da = SETS[n]
        for h in range(2):
            s = ag_send.at[h, i, 1]
            settle(blk(h, g, da, 1, c, w), ag_p2.at[h, i, n, 0])
            send(blk(h, g, da, 1, c, hw), blk(h, g, da, 3, c, hw), s, ag_p2.at[h, i, n, 2], near(h, "b", 1))
            settle(blk(h, g, da, 2, c, w), ag_p2.at[h, i, n, 1])
            send(blk(h, g, da, 2, c + hw, hw), blk(h, g, da, 3, c + hw, hw), s, ag_p2.at[h, i, n, 3], near(h, "b", -1))

    def gathered(i):
        g, c, w = GATHERS[i]
        hw = w // 2
        if i == 0:
            big[0].wait()
            big[1].wait()
        for h in range(2):
            for n in range(3):
                settle(blk(h, g, SETS[n], 3, c, hw), ag_p2.at[h, i, n, 2])
                settle(blk(h, g, SETS[n], 3, c + hw, hw), ag_p2.at[h, i, n, 3])
        for h in range(2):
            v = jnp.dot(
                x[h, g, :, :, :, pl.ds(c, w)].reshape(slots, w),
                w1[pl.ds(h * half + c, w), :],
                preferred_element_type=F32,
            )
            if c == 0 and h == 0:
                acc[g] = v
            else:
                acc[g] += v

    def hide(g):
        gv, uv = acc[g, :, 0:width], acc[g, :, width : 2 * width]
        hid[g] = (gv / (1.0 + jnp.exp(-gv)) * uv).astype(BF16)
        if g == 0:
            big[2].wait()

    def add(ref, index, more):
        ref[index] = (ref[index].astype(F32) + more.astype(F32)).astype(BF16)

    def multiply(i):
        g, c, w = REDUCES[i]
        hw = w // 2
        lo, hi = pl.ds(c, hw), pl.ds(c + hw, hw)
        for h in range(2):
            for t in range(c, c + w, 256):
                v = jnp.dot(hid[g], w2[:, pl.ds(h * half + t, 256)], preferred_element_type=F32)
                v = v.astype(BF16).reshape(SIDE, SIDE, hr, 256)
                if h == 1:
                    part[h, g, :, :, :, pl.ds(t, 256)] = v
                else:
                    for da in range(SIDE):
                        for db in range(SIDE):
                            part[h, g, db, da, :, pl.ds(t, 256)] = v[da, db]
            s = rs_send.at[h, i, 0]
            send(part.at[h, g, 3, :, :, lo], r1.at[h, g, :, :, lo], s, rs_p1.at[h, i, 0], near(h, "b", -1))
            send(part.at[h, g, 3, :, :, hi], r1.at[h, g, :, :, hi], s, rs_p1.at[h, i, 1], near(h, "b", 1))
            send(part.at[h, g, 1, :, :, hi], f1.at[h, g, 0, :, :, hi], s, rs_p1.at[h, i, 2], near(h, "b", -1))
            send(part.at[h, g, 2, :, :, lo], f1.at[h, g, 1, :, :, lo], s, rs_p1.at[h, i, 3], near(h, "b", 1))

    def first_on(i):
        g, c, w = REDUCES[i]
        hw = w // 2
        lo, hi = pl.ds(c, hw), pl.ds(c + hw, hw)
        for h in range(2):
            s = rs_send.at[h, i, 0]
            settle(r1.at[h, g, :, :, lo], rs_p1.at[h, i, 0])
            add(part, (h, g, 1, slice(None), slice(None), lo), r1[h, g, :, :, lo])
            send(part.at[h, g, 1, :, :, lo], f1.at[h, g, 0, :, :, lo], s, rs_p1.at[h, i, 4], near(h, "b", -1))
            settle(r1.at[h, g, :, :, hi], rs_p1.at[h, i, 1])
            add(part, (h, g, 2, slice(None), slice(None), hi), r1[h, g, :, :, hi])
            send(part.at[h, g, 2, :, :, hi], f1.at[h, g, 1, :, :, hi], s, rs_p1.at[h, i, 5], near(h, "b", 1))

    def first_end(i):
        g, c, w = REDUCES[i]
        hw = w // 2
        at, lo, hi = pl.ds(c, w), pl.ds(c, hw), pl.ds(c + hw, hw)
        for h in range(2):
            settle(f1.at[h, g, 0, :, :, hi], rs_p1.at[h, i, 2])
            settle(f1.at[h, g, 1, :, :, lo], rs_p1.at[h, i, 3])
            settle(f1.at[h, g, 0, :, :, lo], rs_p1.at[h, i, 4])
            settle(f1.at[h, g, 1, :, :, hi], rs_p1.at[h, i, 5])
            red[h, g, :, :, at] = (
                part[h, g, 0, :, :, at].astype(F32)
                + f1[h, g, 0, :, :, at].astype(F32)
                + f1[h, g, 1, :, :, at].astype(F32)
            ).astype(BF16)
            s = rs_send.at[h, i, 1]
            send(red.at[h, g, 3, :, lo], r2.at[h, g, :, lo], s, rs_p2.at[h, i, 0], near(h, "a", -1))
            send(red.at[h, g, 3, :, hi], r2.at[h, g, :, hi], s, rs_p2.at[h, i, 1], near(h, "a", 1))
            send(red.at[h, g, 1, :, hi], f2.at[h, g, 0, :, hi], s, rs_p2.at[h, i, 2], near(h, "a", -1))
            send(red.at[h, g, 2, :, lo], f2.at[h, g, 1, :, lo], s, rs_p2.at[h, i, 3], near(h, "a", 1))

    def second_on(i):
        g, c, w = REDUCES[i]
        hw = w // 2
        lo, hi = pl.ds(c, hw), pl.ds(c + hw, hw)
        for h in range(2):
            s = rs_send.at[h, i, 1]
            settle(r2.at[h, g, :, lo], rs_p2.at[h, i, 0])
            add(red, (h, g, 1, slice(None), lo), r2[h, g, :, lo])
            send(red.at[h, g, 1, :, lo], f2.at[h, g, 0, :, lo], s, rs_p2.at[h, i, 4], near(h, "a", -1))
            settle(r2.at[h, g, :, hi], rs_p2.at[h, i, 1])
            add(red, (h, g, 2, slice(None), hi), r2[h, g, :, hi])
            send(red.at[h, g, 2, :, hi], f2.at[h, g, 1, :, hi], s, rs_p2.at[h, i, 5], near(h, "a", 1))

    def second_end(i):
        g, c, w = REDUCES[i]
        hw = w // 2
        at, lo, hi = pl.ds(c, w), pl.ds(c, hw), pl.ds(c + hw, hw)
        weight = jax.nn.sigmoid(jnp.sum(score[g * hr : (g + 1) * hr, :], axis=1, keepdims=True))
        for h in range(2):
            settle(f2.at[h, g, 0, :, hi], rs_p2.at[h, i, 2])
            settle(f2.at[h, g, 1, :, lo], rs_p2.at[h, i, 3])
            settle(f2.at[h, g, 0, :, lo], rs_p2.at[h, i, 4])
            settle(f2.at[h, g, 1, :, hi], rs_p2.at[h, i, 5])
            v = red[h, g, 0, :, at].astype(F32) + f2[h, g, 0, :, at].astype(F32) + f2[h, g, 1, :, at].astype(F32)
            res[h, g * hr : (g + 1) * hr, at] = (v * weight).astype(BF16)

    def give_back(i):
        c, w = RETURNS[i]
        at = pl.ds(c, w)
        both = jnp.concatenate([res[0, :, at], res[1, :, at]], axis=0)
        back = jnp.dot(unpack_m, both, preferred_element_type=F32)
        ro[:, :, at] = back.astype(BF16).reshape(GROUP, 16, w)
        for o in (4, 3, 5, 2, 6, 7, 1):
            to = lax.rem(e + o, GROUP)
            send(ro.at[to, :, at], rr.at[e, :, at], ret_send.at[i], ret_recv.at[i], other(o))
        rr[e, :, at] = ro[e, :, at]

    def out_copy(i, h):
        c, w = RETURNS[i]
        return pltpu.make_async_copy(
            ob.at[h, :, pl.ds(c, w)], out.at[:, pl.ds(h * half + c, w)], out_sem.at[h, i]
        )

    def finish(i):
        c, w = RETURNS[i]
        at = pl.ds(c, w)
        settle(rr.at[pl.ds(0, GROUP - 1), :, at], ret_recv.at[i])
        v = jnp.dot(mats[0 : 2 * ntok, :], rr[:, :, at].reshape(nslot, w), preferred_element_type=F32)
        t = tok[:, :, at].reshape(2 * ntok, w).astype(F32)
        ob[:, :, at] = (t + v).astype(BF16).reshape(2, ntok, w)
        for h in range(2):
            out_copy(i, h).start()

    norm(0)
    norm(1)
    load_weights()
    norm(2)
    clear()
    packing(0)
    own(0)
    own2(0)
    packing(1)
    own(4)
    own(1)
    norm(3)
    own2(1)
    own2(4)
    first_hop(0)
    packing(2)
    own(5)
    forward(0, 0)
    own(2)
    own2(2)
    forward(1, 0)
    first_hop(1)
    first_hop(4)
    first_hop(2)
    packing(3)
    own(7)
    own(3)
    forward(2, 0)
    own(6)
    second_hop(0)
    first_hop(5)
    second_hop(2)
    first_hop(3)
    second_hop(1)
    forward(0, 2)
    first_hop(6)
    second_hop(4)
    first_hop(7)
    forward(0, 1)
    own2(3)
    forward(1, 2)
    forward(1, 1)
    forward(2, 2)
    second_hop(6)
    forward(4, 0)
    own2(6)
    gathered(0)
    own2(7)
    second_hop(3)
    gathered(1)
    forward(2, 1)
    forward(3, 1)
    own2(5)
    second_hop(5)
    second_hop(7)
    forward(3, 0)
    forward(3, 2)
    forward(7, 1)
    forward(4, 1)
    forward(6, 0)
    gathered(2)
    forward(5, 0)
    forward(7, 0)
    forward(5, 2)
    forward(4, 2)
    forward(6, 1)
    forward(6, 2)
    forward(5, 1)
    forward(7, 2)
    gathered(3)
    hide(0)
    multiply(2)
    gathered(4)
    multiply(1)
    gathered(5)
    gathered(6)
    multiply(0)
    first_on(1)
    gathered(7)
    multiply(3)
    first_on(0)
    hide(1)
    multiply(4)
    multiply(5)
    first_on(2)
    first_on(4)
    first_on(5)
    multiply(6)
    first_end(4)
    first_end(0)
    first_end(5)
    first_on(6)
    first_end(1)
    multiply(7)
    second_on(4)
    second_on(0)
    second_on(5)
    first_end(2)
    first_on(3)
    first_on(7)
    second_end(4)
    second_end(0)
    second_on(1)
    first_end(6)
    give_back(0)
    first_end(3)
    second_on(2)
    second_end(5)
    first_end(7)
    second_end(1)
    second_on(6)
    give_back(1)
    second_end(2)
    second_on(3)
    second_on(7)
    second_end(6)
    give_back(2)
    second_end(3)
    second_end(7)
    give_back(3)
    finish(1)
    finish(0)
    finish(2)
    finish(3)

    for i, (g, c, w) in enumerate(GATHERS):
        for h in range(2):
            settle(x.at[h, g, 0, pl.ds(0, 3), :, pl.ds(c, w)], ag_send.at[h, i, 0])
            settle(x.at[h, g, pl.ds(0, 3), :, :, pl.ds(c, w)], ag_send.at[h, i, 1])
    for i, (g, c, w) in enumerate(REDUCES):
        for h in range(2):
            settle(part.at[h, g, pl.ds(0, 3), :, :, pl.ds(c, w)], rs_send.at[h, i, 0])
            settle(red.at[h, g, pl.ds(0, 3), :, pl.ds(c, w)], rs_send.at[h, i, 1])
    for i, (c, w) in enumerate(EXCHANGES):
        settle(so.at[pl.ds(0, GROUP - 1), :, pl.ds(c, w)], a2a_send.at[i])
    for i, (c, w) in enumerate(RETURNS):
        settle(ro.at[pl.ds(0, GROUP - 1), :, pl.ds(c, w)], ret_send.at[i])
        for h in range(2):
            out_copy(i, h).wait()


def shards(tokens, modality, norm_gain, picks, counts, router, gate_weight, up_weight, down_weight):
    ntok, d = tokens.shape
    half = d // 2
    hidden = gate_weight.shape[2]
    rows = GROUP * picks.shape[2] // 2
    hr = rows // 2
    vmem = pl.BlockSpec(memory_space=pltpu.VMEM)
    anywhere = pl.BlockSpec(memory_space=pl.ANY)
    dma = pltpu.SemaphoreType.DMA
    slots = hr * SIDE * SIDE
    ne, ng, nr, nb = len(EXCHANGES), len(GATHERS), len(REDUCES), len(RETURNS)
    return pl.pallas_call(
        kernel,
        name="expert_layer",
        out_shape=jax.ShapeDtypeStruct((ntok, d), BF16),
        in_specs=[anywhere, vmem, vmem, vmem, vmem, anywhere, anywhere, anywhere],
        out_specs=anywhere,
        scratch_shapes=[
            pltpu.VMEM((2, ntok, half), BF16),
            pltpu.VMEM((d, 2 * hidden), BF16),
            pltpu.VMEM((hidden, d), BF16),
            pltpu.VMEM((GROUP, 16, half), BF16),
            pltpu.VMEM((GROUP, 16, half), BF16),
            pltpu.VMEM((2, 2, SIDE, SIDE, hr, half), BF16),
            pltpu.VMEM((2, slots, 2 * hidden), F32),
            pltpu.VMEM((2, slots, hidden), BF16),
            pltpu.VMEM((2, 2, SIDE, SIDE, hr, half), BF16),
            pltpu.VMEM((2, 2, SIDE, hr, half), BF16),
            pltpu.VMEM((2, 2, 2, SIDE, hr, half), BF16),
            pltpu.VMEM((2, 2, SIDE, hr, half), BF16),
            pltpu.VMEM((2, 2, hr, half), BF16),
            pltpu.VMEM((2, 2, 2, hr, half), BF16),
            pltpu.VMEM((2, rows, half), BF16),
            pltpu.VMEM((GROUP, 16, half), BF16),
            pltpu.VMEM((GROUP, 16, half), BF16),
            pltpu.VMEM((2, ntok, half), BF16),
            pltpu.VMEM((rows, 128), F32),
            pltpu.VMEM((2 * ntok + 2 * rows, GROUP * 16), BF16),
            dma((5,)),
            dma((ne,)),
            dma((ne,)),
            dma((2, ng, 2)),
            dma((2, ng, 4)),
            dma((2, ng, 3, 4)),
            dma((2, nr, 2)),
            dma((2, nr, 6)),
            dma((2, nr, 6)),
            dma((nb,)),
            dma((nb,)),
            dma((2, nb)),
        ],
        compiler_params=pltpu.CompilerParams(
            collective_id=0, has_side_effects=True, vmem_limit_bytes=60 * 2**20
        ),
        cost_estimate=pl.CostEstimate(
            flops=12 * slots * d * hidden, bytes_accessed=16 * 2**20, transcendentals=2 * slots * hidden
        ),
    )(tokens, norm_gain, picks, counts, router, gate_weight, up_weight, down_weight)


def solution(mesh):
    placed = (
        P(("dp", "expert"), None),
        P(("dp", "expert")),
        P(),
        P(None, ("dp", "expert"), None),
        P(),
        P("expert", None),
        P("expert", None, "dp"),
        P("expert", None, "dp"),
        P("expert", "dp", None),
    )
    return jax.shard_map(
        shards, mesh=mesh, in_specs=placed, out_specs=P(("dp", "expert"), None), check_vma=False
    )
```

```python
import functools

import jax
import jax.numpy as jnp
from jax import lax
from jax.experimental import pallas as pl
from jax.experimental.pallas import tpu as pltpu
from jax.sharding import PartitionSpec as P

EPSILON = 1e-05
MESH = pl.DeviceIdType.MESH
SIDE = 4
GROUP = 8
F32 = jnp.float32
BF16 = jnp.bfloat16
NEAR = pl.ds(1, 2)
EXCHANGES = ((0, 512), (512, 512), (1024, 1024), (2048, 2048))
GATHERS = ((0, 0, 512), (0, 512, 512), (0, 1024, 1024), (0, 2048, 2048), (1, 0, 1024), (1, 1024, 1024), (1, 2048, 1024), (1, 3072, 1024))
REDUCES = ((0, 0, 1024), (0, 1024, 1024), (0, 2048, 1024), (0, 3072, 1024), (1, 0, 1024), (1, 1024, 1024), (1, 2048, 1024), (1, 3072, 1024))
RETURNS = ((0, 1024), (1024, 1024), (2048, 1024), (3072, 1024))


def iota(shape, dim):
    return lax.broadcasted_iota(jnp.int32, shape, dim)


def kernel(
    tokens, gain_in, picks_in, counts_in, router_in, gate, up, down, out,
    gain, picks, counts, router, tok, w1, w2, so, sr, x, acc, hid, part, r1, f1, red, r2, f2, res, ro, rr, ob, score, mats,
    local_sem, a2a_send, a2a_recv, ag_send, ag_p1, ag_p2, ag_end, rs_send, rs_p1, rs_p2, ret_send, ret_recv, out_sem,
):
    dp, e = lax.axis_index("dp"), lax.axis_index("expert")
    y, z = dp // SIDE, dp % SIDE
    half = tokens.shape[1] // 2
    ntok = tokens.shape[0]
    hr = x.shape[4]
    rows = 2 * hr
    slots = SIDE * SIDE * hr
    width = gate.shape[2]

    def near(h, axis, step):
        along_y = (h == 0) == (axis == "a")
        if along_y:
            return (lax.rem(y + step + SIDE, SIDE) * SIDE + z, e)
        return (y * SIDE + lax.rem(z + step + SIDE, SIDE), e)

    def other(o):
        return (dp, lax.rem(e + o, GROUP))

    def send(src, dst, ssem, rsem, device):
        pltpu.make_async_remote_copy(
            src_ref=src, dst_ref=dst, send_sem=ssem, recv_sem=rsem, device_id=device, device_id_type=MESH
        ).start()

    def settle(ref, sem):
        pltpu.make_async_copy(ref, ref, sem).wait()

    barrier = pltpu.get_barrier_semaphore()
    for step in (-1, 1):
        for axis in "ab":
            pl.semaphore_signal(barrier, 1, device_id=near(0, axis, step), device_id_type=MESH)
    for o in range(1, GROUP):
        pl.semaphore_signal(barrier, 1, device_id=other(o), device_id_type=MESH)

    for h in range(2):
        pltpu.make_async_copy(tokens.at[:, pl.ds(h * half, half)], tok.at[h], local_sem.at[0]).start()
    small = []
    for i, (src, dst) in enumerate(((picks_in, picks), (counts_in, counts), (gain_in, gain), (router_in, router))):
        cp = pltpu.make_async_copy(src, dst, local_sem.at[3 + i])
        cp.start()
        small.append(cp)
    big = [
        pltpu.make_async_copy(gate.at[0], w1.at[:, pl.ds(0, width)], local_sem.at[1]),
        pltpu.make_async_copy(up.at[0], w1.at[:, pl.ds(width, width)], local_sem.at[1]),
        pltpu.make_async_copy(down.at[0], w2, local_sem.at[2]),
    ]

    nslot = GROUP * 16
    lane = iota((8, nslot), 1)
    lane_e, lane_h, lane_k = lane >> 4, (lane >> 3) & 1, lane & 7
    sub = iota((8, nslot), 0)
    small[0].wait()
    small[1].wait()
    pk = picks[:, 0, :] - (dp * GROUP + e) * ntok
    spread = jnp.zeros((8, nslot), jnp.int32)
    for k in range(8):
        spread = spread + jnp.where(lane_k == k, pk[:, k : k + 1], 0)
    pick_row = jnp.sum(jnp.where(sub == lane_e, spread, 0).astype(F32), axis=0, keepdims=True)
    cnt = jnp.sum(jnp.where(sub == e, counts[...], 0).astype(F32), axis=0, keepdims=True)
    cnt16 = jnp.broadcast_to(cnt, (16, nslot)).astype(BF16)
    src = iota((nslot, nslot), 0) - dp * GROUP
    dst_e = iota((nslot, nslot), 1) >> 4
    same = (src == dst_e).astype(F32).astype(BF16)
    before = ((src >= 0) & (src < dst_e)).astype(F32).astype(BF16)
    cnt_r = jnp.dot(cnt16, same, preferred_element_type=F32)[0:1]
    off_r = jnp.dot(cnt16, before, preferred_element_type=F32)[0:1]
    k_r = lane_k[0:1].astype(F32)
    pos_r = jnp.where(k_r < cnt_r, off_r + k_r, -1.0)

    def placing(n, shift):
        q = iota((2 * n, nslot), 0)
        l = iota((2 * n, nslot), 1)
        return ((q >> shift) == ((l >> 3) & 1)), (q & (n - 1)).astype(F32)

    same_half, t_id = placing(ntok, 7)
    put = jnp.where(same_half & (t_id == pick_row), 1.0, 0.0)
    same_half, p_id = placing(rows, 5)
    pack = jnp.where(same_half & (p_id == pos_r), 1.0, 0.0)
    take_m = put.T.astype(BF16)
    mats[0 : 2 * ntok, :] = put.astype(BF16)
    mats[2 * ntok : 2 * ntok + 2 * rows, :] = pack.astype(BF16)
    unpack_m = pack.T.astype(BF16)

    settle(tok, local_sem.at[0])
    for cp in small[2:]:
        cp.wait()
    total = jnp.zeros((nslot, 128), F32)
    for c in range(0, half, 1024):
        t = tok[:, :, pl.ds(c, 1024)].reshape(2 * ntok, 1024)
        g = jnp.dot(take_m, t, preferred_element_type=F32)
        so[:, :, pl.ds(c, 1024)] = g.astype(BF16).reshape(GROUP, 16, 1024)
        sq = g * g
        for i in range(1024 // 128):
            total = total + sq[:, i * 128 : (i + 1) * 128]
    ss = jnp.broadcast_to(jnp.sum(total, axis=1, keepdims=True), (nslot, 128))
    h_col = (iota((nslot, 128), 0) >> 3) & 1
    pair = jnp.where(h_col == 0, pltpu.roll(ss, nslot - 8, 0), pltpu.roll(ss, 8, 0))
    inv = lax.rsqrt((ss + pair)[:, 0:1] / (2 * half) + EPSILON)
    first = h_col[:, 0:1] == 0
    text = iota((nslot, 1), 0) < nslot // 2

    def norm(i):
        c, w = EXCHANGES[i]
        at = pl.ds(c, w)
        ga = gain[:, at]
        gb = gain[:, pl.ds(half + c, w)]
        gm = jnp.where(
            first,
            jnp.where(text, ga[0:1], ga[1:2]),
            jnp.where(text, gb[0:1], gb[1:2]),
        )
        g = so[:, :, at].reshape(nslot, w).astype(F32)
        so[:, :, at] = (g * inv * gm).astype(BF16).reshape(GROUP, 16, w)
        if i == 0:
            pl.semaphore_wait(barrier, 4 + GROUP - 1)
        for o in (4, 3, 5, 2, 6, 7, 1):
            to = lax.rem(e + o, GROUP)
            send(so.at[to, :, at], sr.at[e, :, at], a2a_send.at[0], a2a_recv.at[i], other(o))
        sr[e, :, at] = so[e, :, at]

    def load_weights():
        for cp in big:
            cp.start()

    def clear():
        score[...] = jnp.zeros_like(score)

    def packing(i):
        c, w = EXCHANGES[i]
        at = pl.ds(c, w)
        settle(sr.at[pl.ds(0, GROUP - 1), :, at], a2a_recv.at[i])
        packed = jnp.dot(
            mats[2 * ntok : 2 * ntok + 2 * rows, :], sr[:, :, at].reshape(nslot, w), preferred_element_type=F32
        )
        both = packed.astype(BF16)
        for h in range(2):
            for g in range(2):
                x[h, g, 0, 0, :, at] = both[h * rows + g * hr : h * rows + (g + 1) * hr]
        prod = packed[0:rows] * router[:, at].astype(F32)
        prod += packed[rows : 2 * rows] * router[:, pl.ds(half + c, w)].astype(F32)
        s = score[...]
        for t in range(w // 128):
            s = s + prod[:, t * 128 : (t + 1) * 128]
        score[...] = s

    def blk(h, g, da, db, c, w):
        if h == 1:
            da, db = db, da
        return x.at[h, g, da, db, :, pl.ds(c, w)]

    SETS = (0, NEAR, 3)

    def second(i, n):
        g, c, w = GATHERS[i]
        da = SETS[n]
        s, r = ag_send.at[1], ag_p2.at[i, n]
        for h in range(2):
            send(blk(h, g, da, 0, c, w), blk(h, g, da, 1, c, w), s, r, near(h, "b", 1))
            send(blk(h, g, da, 0, c, w), blk(h, g, da, 2, c, w), s, r, near(h, "b", -1))

    def own(i):
        g, c, w = GATHERS[i]
        s, r = ag_send.at[0], ag_p1.at[i, 0]
        for h in range(2):
            send(blk(h, g, 0, 0, c, w), blk(h, g, 1, 0, c, w), s, r, near(h, "a", 1))
            send(blk(h, g, 0, 0, c, w), blk(h, g, 2, 0, c, w), s, r, near(h, "a", -1))

    def own2(i):
        second(i, 0)

    def first_hop(i):
        g, c, w = GATHERS[i]
        hw = w // 2
        s, r = ag_send.at[0], ag_p1.at[i, 1]
        settle(x.at[0, g, 0, :, :, pl.ds(c, w)], ag_p1.at[i, 0])
        for h in range(2):
            send(blk(h, g, 1, 0, c, hw), blk(h, g, 3, 0, c, hw), s, r, near(h, "a", 1))
            send(blk(h, g, 2, 0, c + hw, hw), blk(h, g, 3, 0, c + hw, hw), s, r, near(h, "a", -1))
        second(i, 1)

    def second_hop(i):
        g, c, w = GATHERS[i]
        settle(x.at[0, g, 0, pl.ds(0, 2), :, pl.ds(c, w)], ag_p1.at[i, 1])
        second(i, 2)

    def forward(i, n):
        g, c, w = GATHERS[i]
        hw = w // 2
        da = SETS[n]
        s, r = ag_send.at[1], ag_end.at[i]
        settle(x.at[0, g, pl.ds(0, 2 if n == 1 else 1), :, :, pl.ds(c, w)], ag_p2.at[i, n])
        for h in range(2):
            send(blk(h, g, da, 1, c, hw), blk(h, g, da, 3, c, hw), s, r, near(h, "b", 1))
            send(blk(h, g, da, 2, c + hw, hw), blk(h, g, da, 3, c + hw, hw), s, r, near(h, "b", -1))

    def gathered(i):
        g, c, w = GATHERS[i]
        if i == 0:
            settle(w1, local_sem.at[1])
        settle(x.at[0, g, pl.ds(0, 2), :, :, pl.ds(c, w)], ag_end.at[i])
        for h in range(2):
            v = jnp.dot(
                x[h, g, :, :, :, pl.ds(c, w)].reshape(slots, w),
                w1[pl.ds(h * half + c, w), :],
                preferred_element_type=F32,
            )
            if c == 0 and h == 0:
                acc[g] = v
            else:
                acc[g] += v

    def hide(g):
        gv, uv = acc[g, :, 0:width], acc[g, :, width : 2 * width]
        hid[g] = (gv / (1.0 + jnp.exp(-gv)) * uv).astype(BF16)
        if g == 0:
            settle(w2, local_sem.at[2])

    def add(ref, index, more):
        ref[index] = (ref[index].astype(F32) + more.astype(F32)).astype(BF16)

    def multiply(i):
        g, c, w = REDUCES[i]
        hw = w // 2
        lo, hi = pl.ds(c, hw), pl.ds(c + hw, hw)
        for h in range(2):
            for t in range(c, c + w, 256):
                v = jnp.dot(hid[g], w2[:, pl.ds(h * half + t, 256)], preferred_element_type=F32)
                v = v.astype(BF16).reshape(SIDE, SIDE, hr, 256)
                if h == 1:
                    part[h, g, :, :, :, pl.ds(t, 256)] = v
                else:
                    for da in range(SIDE):
                        for db in range(SIDE):
                            part[h, g, db, da, :, pl.ds(t, 256)] = v[da, db]
            s = rs_send.at[0]
            send(part.at[h, g, 3, :, :, lo], r1.at[h, g, :, :, lo], s, rs_p1.at[i, 0], near(h, "b", -1))
            send(part.at[h, g, 3, :, :, hi], r1.at[h, g, :, :, hi], s, rs_p1.at[i, 0], near(h, "b", 1))
            send(part.at[h, g, 1, :, :, hi], f1.at[h, g, 0, :, :, hi], s, rs_p1.at[i, 1], near(h, "b", -1))
            send(part.at[h, g, 2, :, :, lo], f1.at[h, g, 1, :, :, lo], s, rs_p1.at[i, 1], near(h, "b", 1))

    def first_on(i):
        g, c, w = REDUCES[i]
        hw = w // 2
        lo, hi = pl.ds(c, hw), pl.ds(c + hw, hw)
        s = rs_send.at[0]
        settle(r1.at[:, g, :, :, pl.ds(c, w)], rs_p1.at[i, 0])
        for h in range(2):
            add(part, (h, g, 1, slice(None), slice(None), lo), r1[h, g, :, :, lo])
            send(part.at[h, g, 1, :, :, lo], f1.at[h, g, 0, :, :, lo], s, rs_p1.at[i, 1], near(h, "b", -1))
            add(part, (h, g, 2, slice(None), slice(None), hi), r1[h, g, :, :, hi])
            send(part.at[h, g, 2, :, :, hi], f1.at[h, g, 1, :, :, hi], s, rs_p1.at[i, 1], near(h, "b", 1))

    def first_end(i):
        g, c, w = REDUCES[i]
        hw = w // 2
        at, lo, hi = pl.ds(c, w), pl.ds(c, hw), pl.ds(c + hw, hw)
        settle(f1.at[:, g, :, :, :, at], rs_p1.at[i, 1])
        for h in range(2):
            red[h, g, :, :, at] = (
                part[h, g, 0, :, :, at].astype(F32)
                + f1[h, g, 0, :, :, at].astype(F32)
                + f1[h, g, 1, :, :, at].astype(F32)
            ).astype(BF16)
            s = rs_send.at[1]
            send(red.at[h, g, 3, :, lo], r2.at[h, g, :, lo], s, rs_p2.at[i, 0], near(h, "a", -1))
            send(red.at[h, g, 3, :, hi], r2.at[h, g, :, hi], s, rs_p2.at[i, 0], near(h, "a", 1))
            send(red.at[h, g, 1, :, hi], f2.at[h, g, 0, :, hi], s, rs_p2.at[i, 1], near(h, "a", -1))
            send(red.at[h, g, 2, :, lo], f2.at[h, g, 1, :, lo], s, rs_p2.at[i, 1], near(h, "a", 1))

    def second_on(i):
        g, c, w = REDUCES[i]
        hw = w // 2
        lo, hi = pl.ds(c, hw), pl.ds(c + hw, hw)
        s = rs_send.at[1]
        settle(r2.at[:, g, :, pl.ds(c, w)], rs_p2.at[i, 0])
        for h in range(2):
            add(red, (h, g, 1, slice(None), lo), r2[h, g, :, lo])
            send(red.at[h, g, 1, :, lo], f2.at[h, g, 0, :, lo], s, rs_p2.at[i, 1], near(h, "a", -1))
            add(red, (h, g, 2, slice(None), hi), r2[h, g, :, hi])
            send(red.at[h, g, 2, :, hi], f2.at[h, g, 1, :, hi], s, rs_p2.at[i, 1], near(h, "a", 1))

    def second_end(i):
        g, c, w = REDUCES[i]
        hw = w // 2
        at, lo, hi = pl.ds(c, w), pl.ds(c, hw), pl.ds(c + hw, hw)
        weight = jax.nn.sigmoid(jnp.sum(score[g * hr : (g + 1) * hr, :], axis=1, keepdims=True))
        settle(f2.at[:, g, :, :, at], rs_p2.at[i, 1])
        for h in range(2):
            v = red[h, g, 0, :, at].astype(F32) + f2[h, g, 0, :, at].astype(F32) + f2[h, g, 1, :, at].astype(F32)
            res[h, g * hr : (g + 1) * hr, at] = (v * weight).astype(BF16)

    def give_back(i):
        c, w = RETURNS[i]
        at = pl.ds(c, w)
        both = jnp.concatenate([res[0, :, at], res[1, :, at]], axis=0)
        back = jnp.dot(unpack_m, both, preferred_element_type=F32)
        ro[:, :, at] = back.astype(BF16).reshape(GROUP, 16, w)
        for o in (4, 3, 5, 2, 6, 7, 1):
            to = lax.rem(e + o, GROUP)
            send(ro.at[to, :, at], rr.at[e, :, at], ret_send.at[0], ret_recv.at[i], other(o))
        rr[e, :, at] = ro[e, :, at]

    def out_copy(i, h):
        c, w = RETURNS[i]
        return pltpu.make_async_copy(
            ob.at[h, :, pl.ds(c, w)], out.at[:, pl.ds(h * half + c, w)], out_sem.at[0]
        )

    def finish(i):
        c, w = RETURNS[i]
        at = pl.ds(c, w)
        settle(rr.at[pl.ds(0, GROUP - 1), :, at], ret_recv.at[i])
        v = jnp.dot(mats[0 : 2 * ntok, :], rr[:, :, at].reshape(nslot, w), preferred_element_type=F32)
        t = tok[:, :, at].reshape(2 * ntok, w).astype(F32)
        ob[:, :, at] = (t + v).astype(BF16).reshape(2, ntok, w)
        for h in range(2):
            out_copy(i, h).start()

    norm(0)
    norm(1)
    load_weights()
    norm(2)
    clear()
    packing(0)
    own(0)
    own2(0)
    packing(1)
    own(4)
    own(1)
    norm(3)
    own2(1)
    own2(4)
    first_hop(0)
    packing(2)
    own(5)
    forward(0, 0)
    own(2)
    own2(2)
    forward(1, 0)
    first_hop(1)
    first_hop(4)
    first_hop(2)
    packing(3)
    own(7)
    own(3)
    forward(2, 0)
    own(6)
    second_hop(0)
    first_hop(5)
    second_hop(2)
    first_hop(3)
    second_hop(1)
    forward(0, 2)
    first_hop(6)
    second_hop(4)
    first_hop(7)
    forward(0, 1)
    own2(3)
    forward(1, 2)
    forward(1, 1)
    forward(2, 2)
    second_hop(6)
    forward(4, 0)
    own2(6)
    gathered(0)
    own2(7)
    second_hop(3)
    gathered(1)
    forward(2, 1)
    forward(3, 1)
    own2(5)
    second_hop(5)
    second_hop(7)
    forward(3, 0)
    forward(3, 2)
    forward(7, 1)
    forward(4, 1)
    forward(6, 0)
    gathered(2)
    forward(5, 0)
    forward(7, 0)
    forward(5, 2)
    forward(4, 2)
    forward(6, 1)
    forward(6, 2)
    forward(5, 1)
    forward(7, 2)
    gathered(3)
    hide(0)
    multiply(2)
    gathered(4)
    multiply(1)
    gathered(5)
    gathered(6)
    multiply(0)
    first_on(1)
    gathered(7)
    multiply(3)
    first_on(0)
    hide(1)
    multiply(4)
    multiply(5)
    first_on(2)
    first_on(4)
    first_on(5)
    multiply(6)
    first_end(4)
    first_end(0)
    first_end(5)
    first_on(6)
    first_end(1)
    multiply(7)
    second_on(4)
    second_on(0)
    second_on(5)
    first_end(2)
    first_on(3)
    first_on(7)
    second_end(4)
    second_end(0)
    second_on(1)
    first_end(6)
    give_back(0)
    first_end(3)
    second_on(2)
    second_end(5)
    first_end(7)
    second_end(1)
    second_on(6)
    give_back(1)
    second_end(2)
    second_on(3)
    second_on(7)
    second_end(6)
    give_back(2)
    second_end(3)
    second_end(7)
    give_back(3)
    finish(1)
    finish(0)
    finish(2)
    finish(3)

    settle(x.at[:, :, 0, pl.ds(0, 3)], ag_send.at[0])
    settle(x.at[:, :, pl.ds(0, 3)], ag_send.at[1])
    settle(part.at[:, :, pl.ds(0, 3)], rs_send.at[0])
    settle(red.at[:, :, pl.ds(0, 3)], rs_send.at[1])
    settle(so.at[pl.ds(0, GROUP - 1)], a2a_send.at[0])
    settle(ro.at[pl.ds(0, GROUP - 1)], ret_send.at[0])
    settle(ob, out_sem.at[0])


def shards(tokens, modality, norm_gain, picks, counts, router, gate_weight, up_weight, down_weight):
    ntok, d = tokens.shape
    half = d // 2
    hidden = gate_weight.shape[2]
    rows = GROUP * picks.shape[2] // 2
    hr = rows // 2
    anywhere = pl.BlockSpec(memory_space=pl.ANY)
    dma = pltpu.SemaphoreType.DMA
    slots = hr * SIDE * SIDE
    ne, ng, nr, nb = len(EXCHANGES), len(GATHERS), len(REDUCES), len(RETURNS)
    return pl.pallas_call(
        kernel,
        name="expert_layer",
        out_shape=jax.ShapeDtypeStruct((ntok, d), BF16),
        in_specs=[anywhere] * 8,
        out_specs=anywhere,
        scratch_shapes=[
            pltpu.VMEM(norm_gain.shape, F32),
            pltpu.VMEM(picks.shape, jnp.int32),
            pltpu.VMEM(counts.shape, jnp.int32),
            pltpu.VMEM(router.shape, BF16),
            pltpu.VMEM((2, ntok, half), BF16),
            pltpu.VMEM((d, 2 * hidden), BF16),
            pltpu.VMEM((hidden, d), BF16),
            pltpu.VMEM((GROUP, 16, half), BF16),
            pltpu.VMEM((GROUP, 16, half), BF16),
            pltpu.VMEM((2, 2, SIDE, SIDE, hr, half), BF16),
            pltpu.VMEM((2, slots, 2 * hidden), F32),
            pltpu.VMEM((2, slots, hidden), BF16),
            pltpu.VMEM((2, 2, SIDE, SIDE, hr, half), BF16),
            pltpu.VMEM((2, 2, SIDE, hr, half), BF16),
            pltpu.VMEM((2, 2, 2, SIDE, hr, half), BF16),
            pltpu.VMEM((2, 2, SIDE, hr, half), BF16),
            pltpu.VMEM((2, 2, hr, half), BF16),
            pltpu.VMEM((2, 2, 2, hr, half), BF16),
            pltpu.VMEM((2, rows, half), BF16),
            pltpu.VMEM((GROUP, 16, half), BF16),
            pltpu.VMEM((GROUP, 16, half), BF16),
            pltpu.VMEM((2, ntok, half), BF16),
            pltpu.VMEM((rows, 128), F32),
            pltpu.VMEM((2 * ntok + 2 * rows, GROUP * 16), BF16),
            dma((7,)),
            dma((1,)),
            dma((ne,)),
            dma((2,)),
            dma((ng, 2)),
            dma((ng, 3)),
            dma((ng,)),
            dma((2,)),
            dma((nr, 2)),
            dma((nr, 2)),
            dma((1,)),
            dma((nb,)),
            dma((1,)),
        ],
        compiler_params=pltpu.CompilerParams(
            collective_id=0, has_side_effects=True, vmem_limit_bytes=60 * 2**20
        ),
        cost_estimate=pl.CostEstimate(
            flops=12 * slots * d * hidden, bytes_accessed=16 * 2**20, transcendentals=2 * slots * hidden
        ),
    )(tokens, norm_gain, picks, counts, router, gate_weight, up_weight, down_weight)


def solution(mesh):
    placed = (
        P(("dp", "expert"), None),
        P(("dp", "expert")),
        P(),
        P(None, ("dp", "expert"), None),
        P(),
        P("expert", None),
        P("expert", None, "dp"),
        P("expert", None, "dp"),
        P("expert", "dp", None),
    )
    return jax.shard_map(
        shards, mesh=mesh, in_specs=placed, out_specs=P(("dp", "expert"), None), check_vma=False
    )
```

```python
import functools

import jax
import jax.numpy as jnp
from jax import lax
from jax.experimental import pallas as pl
from jax.experimental.pallas import tpu as pltpu
from jax.sharding import PartitionSpec as P

EPSILON = 1e-05
MESH = pl.DeviceIdType.MESH
SIDE = 4
GROUP = 8
PIECES = 2
F32 = jnp.float32
BF16 = jnp.bfloat16
NEAR = pl.ds(1, 2)
EXCHANGES = ((0, 512), (512, 512), (1024, 1024), (2048, 2048))
GATHERS = ((0, 0, 512), (0, 512, 512), (0, 1024, 1024), (0, 2048, 1024), (0, 3072, 1024), (1, 0, 1024), (1, 1024, 1024), (1, 2048, 1024), (1, 3072, 1024))
REDUCES = ((0, 0, 1024), (0, 1024, 1024), (0, 2048, 1024), (0, 3072, 1024), (1, 0, 768), (1, 768, 768), (1, 1536, 768), (1, 2304, 768), (1, 3072, 512), (1, 3584, 512))
RETURNS = ((0, 768), (768, 768), (1536, 768), (2304, 768), (3072, 512), (3584, 512))


def iota(shape, dim):
    return lax.broadcasted_iota(jnp.int32, shape, dim)


def kernel(
    tokens, gain_in, picks_in, counts_in, router_in, gate, up, down, rr, put_out,
    gain, picks, counts, router, tok, w1, w2, so, sr, x, acc, hid, part, r1, f1, red, r2, f2, res, ro, score, mats,
    local_sem, a2a_send, a2a_recv, ag_send, ag_p1, ag_p2, ag_end, rs_send, rs_p1, rs_p2, ret_send, ret_recv,
):
    dp, e = lax.axis_index("dp"), lax.axis_index("expert")
    y, z = dp // SIDE, dp % SIDE
    half = tokens.shape[1] // 2
    ntok = tokens.shape[0]
    hr = x.shape[4]
    rows = 2 * hr
    slots = SIDE * SIDE * hr
    width = gate.shape[2]

    def near(h, axis, step):
        along_y = (h == 0) == (axis == "a")
        if along_y:
            return (lax.rem(y + step + SIDE, SIDE) * SIDE + z, e)
        return (y * SIDE + lax.rem(z + step + SIDE, SIDE), e)

    def other(o):
        return (dp, lax.rem(e + o, GROUP))

    def send(src, dst, ssem, rsem, device):
        pltpu.make_async_remote_copy(
            src_ref=src, dst_ref=dst, send_sem=ssem, recv_sem=rsem, device_id=device, device_id_type=MESH
        ).start()

    def settle(ref, sem):
        pltpu.make_async_copy(ref, ref, sem).wait()

    barrier = pltpu.get_barrier_semaphore()
    for step in (-1, 1):
        for axis in "ab":
            pl.semaphore_signal(barrier, 1, device_id=near(0, axis, step), device_id_type=MESH)
    for o in range(1, GROUP):
        pl.semaphore_signal(barrier, 1, device_id=other(o), device_id_type=MESH)

    for h in range(2):
        pltpu.make_async_copy(tokens.at[:, pl.ds(h * half, half)], tok.at[h], local_sem.at[0]).start()
    small = []
    for i, (src, dst) in enumerate(((picks_in, picks), (counts_in, counts), (gain_in, gain), (router_in, router))):
        cp = pltpu.make_async_copy(src, dst, local_sem.at[3 + i])
        cp.start()
        small.append(cp)
    big = [
        pltpu.make_async_copy(gate.at[0], w1.at[:, pl.ds(0, width)], local_sem.at[1]),
        pltpu.make_async_copy(up.at[0], w1.at[:, pl.ds(width, width)], local_sem.at[1]),
        pltpu.make_async_copy(down.at[0], w2, local_sem.at[2]),
    ]

    nslot = GROUP * 16
    lane = iota((8, nslot), 1)
    lane_e, lane_h, lane_k = lane >> 4, (lane >> 3) & 1, lane & 7
    sub = iota((8, nslot), 0)
    small[0].wait()
    small[1].wait()
    pk = picks[:, 0, :] - (dp * GROUP + e) * ntok
    spread = jnp.zeros((8, nslot), jnp.int32)
    for k in range(8):
        spread = spread + jnp.where(lane_k == k, pk[:, k : k + 1], 0)
    pick_row = jnp.sum(jnp.where(sub == lane_e, spread, 0).astype(F32), axis=0, keepdims=True)
    cnt = jnp.sum(jnp.where(sub == e, counts[...], 0).astype(F32), axis=0, keepdims=True)
    cnt16 = jnp.broadcast_to(cnt, (16, nslot)).astype(BF16)
    src = iota((nslot, nslot), 0) - dp * GROUP
    dst_e = iota((nslot, nslot), 1) >> 4
    same = (src == dst_e).astype(F32).astype(BF16)
    before = ((src >= 0) & (src < dst_e)).astype(F32).astype(BF16)
    cnt_r = jnp.dot(cnt16, same, preferred_element_type=F32)[0:1]
    off_r = jnp.dot(cnt16, before, preferred_element_type=F32)[0:1]
    k_r = lane_k[0:1].astype(F32)
    pos_r = jnp.where(k_r < cnt_r, off_r + k_r, -1.0)

    def placing(n, shift):
        q = iota((2 * n, nslot), 0)
        l = iota((2 * n, nslot), 1)
        return ((q >> shift) == ((l >> 3) & 1)), (q & (n - 1)).astype(F32)

    same_half, t_id = placing(ntok, 7)
    put = jnp.where(same_half & (t_id == pick_row), 1.0, 0.0)
    same_half, p_id = placing(rows, 5)
    pack = jnp.where(same_half & (p_id == pos_r), 1.0, 0.0)
    take_m = put.T.astype(BF16)
    mats[0 : 2 * ntok, :] = put.astype(BF16)
    mats[2 * ntok : 2 * ntok + 2 * rows, :] = pack.astype(BF16)
    put_copy = pltpu.make_async_copy(mats.at[pl.ds(0, 2 * ntok)], put_out, local_sem.at[7])
    put_copy.start()
    unpack_m = pack.T.astype(BF16)

    settle(tok, local_sem.at[0])
    for cp in small[2:]:
        cp.wait()
    total = jnp.zeros((nslot, 128), F32)
    for c in range(0, half, 1024):
        t = tok[:, :, pl.ds(c, 1024)].reshape(2 * ntok, 1024)
        g = jnp.dot(take_m, t, preferred_element_type=F32)
        so[:, :, pl.ds(c, 1024)] = g.astype(BF16).reshape(GROUP, 16, 1024)
        sq = g * g
        for i in range(1024 // 128):
            total = total + sq[:, i * 128 : (i + 1) * 128]
    ss = jnp.broadcast_to(jnp.sum(total, axis=1, keepdims=True), (nslot, 128))
    h_col = (iota((nslot, 128), 0) >> 3) & 1
    pair = jnp.where(h_col == 0, pltpu.roll(ss, nslot - 8, 0), pltpu.roll(ss, 8, 0))
    inv = lax.rsqrt((ss + pair)[:, 0:1] / (2 * half) + EPSILON)
    first = h_col[:, 0:1] == 0
    text = iota((nslot, 1), 0) < nslot // 2

    def norm(i):
        c, w = EXCHANGES[i]
        at = pl.ds(c, w)
        ga = gain[:, at]
        gb = gain[:, pl.ds(half + c, w)]
        gm = jnp.where(
            first,
            jnp.where(text, ga[0:1], ga[1:2]),
            jnp.where(text, gb[0:1], gb[1:2]),
        )
        g = so[:, :, at].reshape(nslot, w).astype(F32)
        so[:, :, at] = (g * inv * gm).astype(BF16).reshape(GROUP, 16, w)
        if i == 0:
            pl.semaphore_wait(barrier, 4 + GROUP - 1)
        for o in (4, 3, 5, 2, 6, 7, 1):
            to = lax.rem(e + o, GROUP)
            send(so.at[to, :, at], sr.at[e, :, at], a2a_send.at[0], a2a_recv.at[i], other(o))
        sr[e, :, at] = so[e, :, at]

    def load_weights():
        for cp in big:
            cp.start()

    def clear():
        score[...] = jnp.zeros_like(score)

    def packing(i):
        c, w = EXCHANGES[i]
        at = pl.ds(c, w)
        settle(sr.at[pl.ds(0, GROUP - 1), :, at], a2a_recv.at[i])
        packed = jnp.dot(
            mats[2 * ntok : 2 * ntok + 2 * rows, :], sr[:, :, at].reshape(nslot, w), preferred_element_type=F32
        )
        both = packed.astype(BF16)
        for h in range(2):
            for g in range(2):
                x[h, g, 0, 0, :, at] = both[h * rows + g * hr : h * rows + (g + 1) * hr]
        prod = packed[0:rows] * router[:, at].astype(F32)
        prod += packed[rows : 2 * rows] * router[:, pl.ds(half + c, w)].astype(F32)
        s = score[...]
        for t in range(w // 128):
            s = s + prod[:, t * 128 : (t + 1) * 128]
        score[...] = s

    def blk(h, g, da, db, c, w):
        if h == 1:
            da, db = db, da
        return x.at[h, g, da, db, :, pl.ds(c, w)]

    SETS = (0, NEAR, 3)

    def second(i, n):
        g, c, w = GATHERS[i]
        da = SETS[n]
        s, r = ag_send.at[1], ag_p2.at[i, n]
        for h in range(2):
            send(blk(h, g, da, 0, c, w), blk(h, g, da, 1, c, w), s, r, near(h, "b", 1))
            send(blk(h, g, da, 0, c, w), blk(h, g, da, 2, c, w), s, r, near(h, "b", -1))

    def own(i):
        g, c, w = GATHERS[i]
        s, r = ag_send.at[0], ag_p1.at[i, 0]
        for h in range(2):
            send(blk(h, g, 0, 0, c, w), blk(h, g, 1, 0, c, w), s, r, near(h, "a", 1))
            send(blk(h, g, 0, 0, c, w), blk(h, g, 2, 0, c, w), s, r, near(h, "a", -1))

    def own2(i):
        second(i, 0)

    def first_hop(i):
        g, c, w = GATHERS[i]
        hw = w // 2
        s, r = ag_send.at[0], ag_p1.at[i, 1]
        settle(x.at[0, g, 0, :, :, pl.ds(c, w)], ag_p1.at[i, 0])
        for h in range(2):
            send(blk(h, g, 1, 0, c, hw), blk(h, g, 3, 0, c, hw), s, r, near(h, "a", 1))
            send(blk(h, g, 2, 0, c + hw, hw), blk(h, g, 3, 0, c + hw, hw), s, r, near(h, "a", -1))
        second(i, 1)

    def second_hop(i):
        g, c, w = GATHERS[i]
        settle(x.at[0, g, 0, pl.ds(0, 2), :, pl.ds(c, w)], ag_p1.at[i, 1])
        second(i, 2)

    def forward(i, n):
        g, c, w = GATHERS[i]
        hw = w // 2
        da = SETS[n]
        s, r = ag_send.at[1], ag_end.at[i]
        settle(x.at[0, g, pl.ds(0, 2 if n == 1 else 1), :, :, pl.ds(c, w)], ag_p2.at[i, n])
        for h in range(2):
            send(blk(h, g, da, 1, c, hw), blk(h, g, da, 3, c, hw), s, r, near(h, "b", 1))
            send(blk(h, g, da, 2, c + hw, hw), blk(h, g, da, 3, c + hw, hw), s, r, near(h, "b", -1))

    def gathered(i):
        g, c, w = GATHERS[i]
        if i == 0:
            settle(w1, local_sem.at[1])
        settle(x.at[0, g, pl.ds(0, 2), :, :, pl.ds(c, w)], ag_end.at[i])
        for h in range(2):
            v = jnp.dot(
                x[h, g, :, :, :, pl.ds(c, w)].reshape(slots, w),
                w1[pl.ds(h * half + c, w), :],
                preferred_element_type=F32,
            )
            if c == 0 and h == 0:
                acc[g] = v
            else:
                acc[g] += v

    def hide(g):
        gv, uv = acc[g, :, 0:width], acc[g, :, width : 2 * width]
        hid[g] = (gv / (1.0 + jnp.exp(-gv)) * uv).astype(BF16)
        if g == 0:
            settle(w2, local_sem.at[2])

    def add(ref, index, more):
        ref[index] = (ref[index].astype(F32) + more.astype(F32)).astype(BF16)

    def multiply(i):
        g, c, w = REDUCES[i]
        hw = w // 2
        lo, hi = pl.ds(c, hw), pl.ds(c + hw, hw)
        for h in range(2):
            for t in range(c, c + w, 256):
                v = jnp.dot(hid[g], w2[:, pl.ds(h * half + t, 256)], preferred_element_type=F32)
                v = v.astype(BF16).reshape(SIDE, SIDE, hr, 256)
                if h == 1:
                    part[h, g, :, :, :, pl.ds(t, 256)] = v
                else:
                    for da in range(SIDE):
                        for db in range(SIDE):
                            part[h, g, db, da, :, pl.ds(t, 256)] = v[da, db]
            s = rs_send.at[0]
            send(part.at[h, g, 3, :, :, lo], r1.at[h, g, :, :, lo], s, rs_p1.at[i, 0], near(h, "b", -1))
            send(part.at[h, g, 3, :, :, hi], r1.at[h, g, :, :, hi], s, rs_p1.at[i, 0], near(h, "b", 1))
            send(part.at[h, g, 1, :, :, hi], f1.at[h, g, 0, :, :, hi], s, rs_p1.at[i, 1], near(h, "b", -1))
            send(part.at[h, g, 2, :, :, lo], f1.at[h, g, 1, :, :, lo], s, rs_p1.at[i, 1], near(h, "b", 1))

    def first_on(i):
        g, c, w = REDUCES[i]
        hw = w // 2
        lo, hi = pl.ds(c, hw), pl.ds(c + hw, hw)
        s = rs_send.at[0]
        settle(r1.at[:, g, :, :, pl.ds(c, w)], rs_p1.at[i, 0])
        for h in range(2):
            add(part, (h, g, 1, slice(None), slice(None), lo), r1[h, g, :, :, lo])
            send(part.at[h, g, 1, :, :, lo], f1.at[h, g, 0, :, :, lo], s, rs_p1.at[i, 1], near(h, "b", -1))
            add(part, (h, g, 2, slice(None), slice(None), hi), r1[h, g, :, :, hi])
            send(part.at[h, g, 2, :, :, hi], f1.at[h, g, 1, :, :, hi], s, rs_p1.at[i, 1], near(h, "b", 1))

    def first_end(i):
        g, c, w = REDUCES[i]
        hw = w // 2
        at, lo, hi = pl.ds(c, w), pl.ds(c, hw), pl.ds(c + hw, hw)
        settle(f1.at[:, g, :, :, :, at], rs_p1.at[i, 1])
        for h in range(2):
            red[h, g, :, :, at] = (
                part[h, g, 0, :, :, at].astype(F32)
                + f1[h, g, 0, :, :, at].astype(F32)
                + f1[h, g, 1, :, :, at].astype(F32)
            ).astype(BF16)
            s = rs_send.at[1]
            send(red.at[h, g, 3, :, lo], r2.at[h, g, :, lo], s, rs_p2.at[i, 0], near(h, "a", -1))
            send(red.at[h, g, 3, :, hi], r2.at[h, g, :, hi], s, rs_p2.at[i, 0], near(h, "a", 1))
            send(red.at[h, g, 1, :, hi], f2.at[h, g, 0, :, hi], s, rs_p2.at[i, 1], near(h, "a", -1))
            send(red.at[h, g, 2, :, lo], f2.at[h, g, 1, :, lo], s, rs_p2.at[i, 1], near(h, "a", 1))

    def second_on(i):
        g, c, w = REDUCES[i]
        hw = w // 2
        lo, hi = pl.ds(c, hw), pl.ds(c + hw, hw)
        s = rs_send.at[1]
        settle(r2.at[:, g, :, pl.ds(c, w)], rs_p2.at[i, 0])
        for h in range(2):
            add(red, (h, g, 1, slice(None), lo), r2[h, g, :, lo])
            send(red.at[h, g, 1, :, lo], f2.at[h, g, 0, :, lo], s, rs_p2.at[i, 1], near(h, "a", -1))
            add(red, (h, g, 2, slice(None), hi), r2[h, g, :, hi])
            send(red.at[h, g, 2, :, hi], f2.at[h, g, 1, :, hi], s, rs_p2.at[i, 1], near(h, "a", 1))

    def second_end(i):
        g, c, w = REDUCES[i]
        hw = w // 2
        at, lo, hi = pl.ds(c, w), pl.ds(c, hw), pl.ds(c + hw, hw)
        weight = jax.nn.sigmoid(jnp.sum(score[g * hr : (g + 1) * hr, :], axis=1, keepdims=True))
        settle(f2.at[:, g, :, :, at], rs_p2.at[i, 1])
        for h in range(2):
            v = red[h, g, 0, :, at].astype(F32) + f2[h, g, 0, :, at].astype(F32) + f2[h, g, 1, :, at].astype(F32)
            res[h, g * hr : (g + 1) * hr, at] = (v * weight).astype(BF16)

    def give_back(i):
        c, w = RETURNS[i]
        at = pl.ds(c, w)
        both = jnp.concatenate([res[0, :, at], res[1, :, at]], axis=0)
        back = jnp.dot(unpack_m, both, preferred_element_type=F32)
        ro[:, :, at] = back.astype(BF16).reshape(GROUP, 16, w)
        for o in (4, 3, 5, 2, 6, 7, 1):
            to = lax.rem(e + o, GROUP)
            send(ro.at[to, :, at], rr.at[e, :, at], ret_send.at[0], ret_recv.at[i], other(o))
        pltpu.make_async_copy(ro.at[e, :, at], rr.at[e, :, at], local_sem.at[8]).start()

    def finish(i):
        c, w = RETURNS[i]
        settle(rr.at[pl.ds(0, GROUP - 1), :, pl.ds(c, w)], ret_recv.at[i])

    norm(0)
    load_weights()
    norm(1)
    norm(2)
    clear()
    packing(0)
    own(0)
    own2(0)
    packing(1)
    own(5)
    own(1)
    norm(3)
    own2(5)
    own2(1)
    first_hop(0)
    packing(2)
    own(2)
    own(6)
    first_hop(5)
    forward(1, 0)
    first_hop(1)
    forward(0, 0)
    first_hop(2)
    packing(3)
    own(4)
    own(7)
    forward(0, 1)
    forward(5, 0)
    own2(3)
    own(3)
    forward(1, 1)
    own2(4)
    second_hop(2)
    own2(7)
    first_hop(4)
    own2(2)
    second_hop(0)
    own(8)
    second_hop(1)
    first_hop(3)
    second_hop(4)
    forward(2, 1)
    forward(2, 0)
    second_hop(5)
    forward(3, 0)
    forward(0, 2)
    forward(2, 2)
    forward(5, 1)
    second_hop(3)
    forward(7, 0)
    first_hop(6)
    forward(1, 2)
    first_hop(7)
    forward(3, 2)
    first_hop(8)
    own2(6)
    forward(3, 1)
    forward(4, 1)
    forward(4, 2)
    own2(8)
    forward(4, 0)
    forward(6, 1)
    second_hop(6)
    forward(8, 1)
    gathered(0)
    gathered(1)
    second_hop(8)
    second_hop(7)
    forward(5, 2)
    forward(7, 1)
    gathered(2)
    gathered(3)
    forward(6, 0)
    gathered(4)
    forward(8, 0)
    hide(0)
    multiply(0)
    multiply(1)
    forward(7, 2)
    forward(8, 2)
    forward(6, 2)
    first_on(0)
    multiply(3)
    gathered(5)
    multiply(2)
    gathered(6)
    gathered(7)
    gathered(8)
    first_on(1)
    hide(1)
    multiply(4)
    multiply(5)
    multiply(6)
    first_on(4)
    first_end(1)
    multiply(8)
    first_end(0)
    first_on(5)
    multiply(7)
    first_end(4)
    first_on(6)
    first_on(2)
    multiply(9)
    first_end(5)
    first_on(7)
    first_end(6)
    first_on(8)
    second_on(4)
    second_on(0)
    first_end(2)
    first_on(3)
    second_on(5)
    second_on(1)
    first_end(7)
    first_on(9)
    second_end(4)
    second_end(0)
    first_end(8)
    second_on(6)
    second_on(2)
    give_back(0)
    first_end(3)
    second_end(5)
    second_end(1)
    give_back(1)
    second_on(7)
    first_end(9)
    second_on(8)
    second_end(6)
    second_end(2)
    give_back(2)
    second_on(3)
    second_end(7)
    give_back(3)
    second_on(9)
    second_end(8)
    second_end(3)
    give_back(4)
    finish(1)
    second_end(9)
    give_back(5)
    finish(2)
    finish(0)
    finish(3)
    finish(4)
    finish(5)

    settle(x.at[:, :, 0, pl.ds(0, 3)], ag_send.at[0])
    settle(x.at[:, :, pl.ds(0, 3)], ag_send.at[1])
    settle(part.at[:, :, pl.ds(0, 3)], rs_send.at[0])
    settle(red.at[:, :, pl.ds(0, 3)], rs_send.at[1])
    settle(so.at[pl.ds(0, GROUP - 1)], a2a_send.at[0])
    settle(ro.at[pl.ds(0, GROUP - 1)], ret_send.at[0])
    settle(ro.at[0], local_sem.at[8])
    put_copy.wait()


def add_returned(tokens, returned, put_in, out, tok, back, put, ob, load_sem, store_sem, put_sem):
    ntok, half = tokens.shape[0], tokens.shape[1] // 2
    w = half // PIECES
    put_copy = pltpu.make_async_copy(put_in, put, put_sem.at[0])
    put_copy.start()
    loads, stores = [], []
    for i in range(PIECES):
        at = pl.ds(i * w, w)
        row = [pltpu.make_async_copy(returned.at[:, :, at], back.at[:, :, at], load_sem.at[i, 2])]
        for h in range(2):
            there = pl.ds(h * half + i * w, w)
            row.append(pltpu.make_async_copy(tokens.at[:, there], tok.at[h, :, at], load_sem.at[i, h]))
        for cp in row:
            cp.start()
        loads.append(row)
    put_copy.wait()
    for i in range(PIECES):
        at = pl.ds(i * w, w)
        for cp in loads[i]:
            cp.wait()
        v = jnp.dot(put[...], back[:, :, at].reshape(GROUP * 16, w), preferred_element_type=F32)
        t = tok[:, :, at].reshape(2 * ntok, w).astype(F32)
        ob[:, :, at] = (t + v).astype(BF16).reshape(2, ntok, w)
        for h in range(2):
            cp = pltpu.make_async_copy(ob.at[h, :, at], out.at[:, pl.ds(h * half + i * w, w)], store_sem.at[i, h])
            cp.start()
            stores.append(cp)
    for cp in stores:
        cp.wait()


def shards(tokens, modality, norm_gain, picks, counts, router, gate_weight, up_weight, down_weight):
    ntok, d = tokens.shape
    half = d // 2
    hidden = gate_weight.shape[2]
    rows = GROUP * picks.shape[2] // 2
    hr = rows // 2
    anywhere = pl.BlockSpec(memory_space=pl.ANY)
    dma = pltpu.SemaphoreType.DMA
    slots = hr * SIDE * SIDE
    ne, ng, nr, nb = len(EXCHANGES), len(GATHERS), len(REDUCES), len(RETURNS)
    returned, put = pl.pallas_call(
        kernel,
        name="expert_layer",
        out_shape=(
            jax.ShapeDtypeStruct((GROUP, 16, half), BF16),
            jax.ShapeDtypeStruct((2 * ntok, GROUP * 16), BF16),
        ),
        in_specs=[anywhere] * 8,
        out_specs=(anywhere, anywhere),
        scratch_shapes=[
            pltpu.VMEM(norm_gain.shape, F32),
            pltpu.VMEM(picks.shape, jnp.int32),
            pltpu.VMEM(counts.shape, jnp.int32),
            pltpu.VMEM(router.shape, BF16),
            pltpu.VMEM((2, ntok, half), BF16),
            pltpu.VMEM((d, 2 * hidden), BF16),
            pltpu.VMEM((hidden, d), BF16),
            pltpu.VMEM((GROUP, 16, half), BF16),
            pltpu.VMEM((GROUP, 16, half), BF16),
            pltpu.VMEM((2, 2, SIDE, SIDE, hr, half), BF16),
            pltpu.VMEM((2, slots, 2 * hidden), F32),
            pltpu.VMEM((2, slots, hidden), BF16),
            pltpu.VMEM((2, 2, SIDE, SIDE, hr, half), BF16),
            pltpu.VMEM((2, 2, SIDE, hr, half), BF16),
            pltpu.VMEM((2, 2, 2, SIDE, hr, half), BF16),
            pltpu.VMEM((2, 2, SIDE, hr, half), BF16),
            pltpu.VMEM((2, 2, hr, half), BF16),
            pltpu.VMEM((2, 2, 2, hr, half), BF16),
            pltpu.VMEM((2, rows, half), BF16),
            pltpu.VMEM((GROUP, 16, half), BF16),
            pltpu.VMEM((rows, 128), F32),
            pltpu.VMEM((2 * ntok + 2 * rows, GROUP * 16), BF16),
            dma((9,)),
            dma((1,)),
            dma((ne,)),
            dma((2,)),
            dma((ng, 2)),
            dma((ng, 3)),
            dma((ng,)),
            dma((2,)),
            dma((nr, 2)),
            dma((nr, 2)),
            dma((1,)),
            dma((nb,)),
        ],
        compiler_params=pltpu.CompilerParams(
            collective_id=0, has_side_effects=True, vmem_limit_bytes=56 * 2**20
        ),
        cost_estimate=pl.CostEstimate(
            flops=12 * slots * d * hidden, bytes_accessed=16 * 2**20, transcendentals=2 * slots * hidden
        ),
    )(tokens, norm_gain, picks, counts, router, gate_weight, up_weight, down_weight)
    return pl.pallas_call(
        add_returned,
        name="add_returned",
        out_shape=jax.ShapeDtypeStruct((ntok, d), BF16),
        in_specs=[anywhere] * 3,
        out_specs=anywhere,
        scratch_shapes=[
            pltpu.VMEM((2, ntok, half), BF16),
            pltpu.VMEM((GROUP, 16, half), BF16),
            pltpu.VMEM((2 * ntok, GROUP * 16), BF16),
            pltpu.VMEM((2, ntok, half), BF16),
            dma((PIECES, 3)),
            dma((PIECES, 2)),
            dma((1,)),
        ],
        compiler_params=pltpu.CompilerParams(vmem_limit_bytes=57 * 2**20),
        cost_estimate=pl.CostEstimate(
            flops=4 * ntok * GROUP * 16 * half, bytes_accessed=5 * ntok * d, transcendentals=0
        ),
    )(tokens, returned, put)


def solution(mesh):
    placed = (
        P(("dp", "expert"), None),
        P(("dp", "expert")),
        P(),
        P(None, ("dp", "expert"), None),
        P(),
        P("expert", None),
        P("expert", None, "dp"),
        P("expert", None, "dp"),
        P("expert", "dp", None),
    )
    return jax.shard_map(
        shards, mesh=mesh, in_specs=placed, out_specs=P(("dp", "expert"), None), check_vma=False
    )
```

```python
import functools

import jax
import jax.numpy as jnp
from jax import lax
from jax.experimental import pallas as pl
from jax.experimental.pallas import tpu as pltpu
from jax.sharding import PartitionSpec as P

EPSILON = 1e-05
MESH = pl.DeviceIdType.MESH
SIDE = 4
GROUP = 8
PIECES = 2
F32 = jnp.float32
BF16 = jnp.bfloat16
NEAR = pl.ds(1, 2)
EXCHANGES = ((0, 512), (512, 512), (1024, 1024), (2048, 2048))
GATHERS = ((0, 0, 512), (0, 512, 512), (0, 1024, 1024), (0, 2048, 2048), (1, 0, 1024), (1, 1024, 1024), (1, 2048, 1024), (1, 3072, 1024))
REDUCES = ((0, 0, 1024), (0, 1024, 1024), (0, 2048, 1024), (0, 3072, 1024), (1, 0, 1024), (1, 1024, 1024), (1, 2048, 1024), (1, 3072, 1024))
RETURNS = ((0, 1024), (1024, 1024), (2048, 1024), (3072, 1024))


def iota(shape, dim):
    return lax.broadcasted_iota(jnp.int32, shape, dim)


def kernel(
    tokens, gain_in, picks_in, counts_in, router_in, gate, up, down, rr, put_out,
    gain, picks, counts, router, tok, w1, w2, so, sr, x, acc, hid, part, r1, f1, red, r2, f2, res, ro, score, mats,
    local_sem, a2a_send, a2a_recv, ag_send, ag_p1, ag_p2, ag_end, rs_send, rs_p1, rs_p2, ret_send, ret_recv,
):
    dp, e = lax.axis_index("dp"), lax.axis_index("expert")
    y, z = dp // SIDE, dp % SIDE
    half = tokens.shape[1] // 2
    ntok = tokens.shape[0]
    hr = x.shape[4]
    rows = 2 * hr
    slots = SIDE * SIDE * hr
    width = gate.shape[2]

    def near(h, axis, step):
        along_y = (h == 0) == (axis == "a")
        if along_y:
            return (lax.rem(y + step + SIDE, SIDE) * SIDE + z, e)
        return (y * SIDE + lax.rem(z + step + SIDE, SIDE), e)

    def other(o):
        return (dp, lax.rem(e + o, GROUP))

    def send(src, dst, ssem, rsem, device):
        pltpu.make_async_remote_copy(
            src_ref=src, dst_ref=dst, send_sem=ssem, recv_sem=rsem, device_id=device, device_id_type=MESH
        ).start()

    def settle(ref, sem):
        pltpu.make_async_copy(ref, ref, sem).wait()

    barrier = pltpu.get_barrier_semaphore()
    for step in (-1, 1):
        for axis in "ab":
            pl.semaphore_signal(barrier, 1, device_id=near(0, axis, step), device_id_type=MESH)
    for o in range(1, GROUP):
        pl.semaphore_signal(barrier, 1, device_id=other(o), device_id_type=MESH)

    for h in range(2):
        pltpu.make_async_copy(tokens.at[:, pl.ds(h * half, half)], tok.at[h], local_sem.at[0]).start()
    small = []
    for i, (src, dst) in enumerate(((picks_in, picks), (counts_in, counts), (gain_in, gain), (router_in, router))):
        cp = pltpu.make_async_copy(src, dst, local_sem.at[3 + i])
        cp.start()
        small.append(cp)
    big = [
        pltpu.make_async_copy(gate.at[0], w1.at[:, pl.ds(0, width)], local_sem.at[1]),
        pltpu.make_async_copy(up.at[0], w1.at[:, pl.ds(width, width)], local_sem.at[1]),
        pltpu.make_async_copy(down.at[0], w2, local_sem.at[2]),
    ]

    nslot = GROUP * 16
    lane = iota((8, nslot), 1)
    lane_e, lane_h, lane_k = lane >> 4, (lane >> 3) & 1, lane & 7
    sub = iota((8, nslot), 0)
    small[0].wait()
    pk = picks[:, 0, :] - (dp * GROUP + e) * ntok
    spread = jnp.zeros((8, nslot), jnp.int32)
    for k in range(8):
        spread = spread + jnp.where(lane_k == k, pk[:, k : k + 1], 0)
    pick_row = jnp.sum(jnp.where(sub == lane_e, spread, 0).astype(F32), axis=0, keepdims=True)
    def placing(n, shift):
        q = iota((2 * n, nslot), 0)
        l = iota((2 * n, nslot), 1)
        return ((q >> shift) == ((l >> 3) & 1)), (q & (n - 1)).astype(F32)

    same_half, t_id = placing(ntok, 7)
    put = jnp.where(same_half & (t_id == pick_row), 1.0, 0.0)
    take_m = put.T.astype(BF16)
    mats[0 : 2 * ntok, :] = put.astype(BF16)
    put_copy = pltpu.make_async_copy(mats.at[pl.ds(0, 2 * ntok)], put_out, local_sem.at[7])
    put_copy.start()

    settle(tok, local_sem.at[0])
    for cp in small[2:]:
        cp.wait()
    total = jnp.zeros((nslot, 128), F32)
    for c in range(0, half, 1024):
        t = tok[:, :, pl.ds(c, 1024)].reshape(2 * ntok, 1024)
        g = jnp.dot(take_m, t, preferred_element_type=F32)
        so[:, :, pl.ds(c, 1024)] = g.astype(BF16).reshape(GROUP, 16, 1024)
        sq = g * g
        for i in range(1024 // 128):
            total = total + sq[:, i * 128 : (i + 1) * 128]
    ss = jnp.broadcast_to(jnp.sum(total, axis=1, keepdims=True), (nslot, 128))
    h_col = (iota((nslot, 128), 0) >> 3) & 1
    pair = jnp.where(h_col == 0, pltpu.roll(ss, nslot - 8, 0), pltpu.roll(ss, 8, 0))
    inv = lax.rsqrt((ss + pair)[:, 0:1] / (2 * half) + EPSILON)
    first = h_col[:, 0:1] == 0
    text = iota((nslot, 1), 0) < nslot // 2

    def norm(i):
        c, w = EXCHANGES[i]
        at = pl.ds(c, w)
        ga = gain[:, at]
        gb = gain[:, pl.ds(half + c, w)]
        gm = jnp.where(
            first,
            jnp.where(text, ga[0:1], ga[1:2]),
            jnp.where(text, gb[0:1], gb[1:2]),
        )
        g = so[:, :, at].reshape(nslot, w).astype(F32)
        so[:, :, at] = (g * inv * gm).astype(BF16).reshape(GROUP, 16, w)
        if i == 0:
            pl.semaphore_wait(barrier, 4 + GROUP - 1)
        for o in (4, 3, 5, 2, 6, 7, 1):
            to = lax.rem(e + o, GROUP)
            send(so.at[to, :, at], sr.at[e, :, at], a2a_send.at[0], a2a_recv.at[i], other(o))
        sr[e, :, at] = so[e, :, at]

    def pack_matrices():
        small[1].wait()
        cnt = jnp.sum(jnp.where(sub == e, counts[...], 0).astype(F32), axis=0, keepdims=True)
        cnt16 = jnp.broadcast_to(cnt, (16, nslot)).astype(BF16)
        src = iota((nslot, nslot), 0) - dp * GROUP
        dst_e = iota((nslot, nslot), 1) >> 4
        same = (src == dst_e).astype(F32).astype(BF16)
        before = ((src >= 0) & (src < dst_e)).astype(F32).astype(BF16)
        cnt_r = jnp.dot(cnt16, same, preferred_element_type=F32)[0:1]
        off_r = jnp.dot(cnt16, before, preferred_element_type=F32)[0:1]
        k_r = lane_k[0:1].astype(F32)
        pos_r = jnp.where(k_r < cnt_r, off_r + k_r, -1.0)
        same_half, p_id = placing(rows, 5)
        pack = jnp.where(same_half & (p_id == pos_r), 1.0, 0.0)
        mats[2 * ntok : 2 * ntok + 2 * rows, :] = pack.astype(BF16)
        unpack_m = pack.T.astype(BF16)
        return unpack_m

    def load_weights():
        for cp in big:
            cp.start()

    def clear():
        score[...] = jnp.zeros_like(score)

    def packing(i):
        c, w = EXCHANGES[i]
        at = pl.ds(c, w)
        settle(sr.at[pl.ds(0, GROUP - 1), :, at], a2a_recv.at[i])
        packed = jnp.dot(
            mats[2 * ntok : 2 * ntok + 2 * rows, :], sr[:, :, at].reshape(nslot, w), preferred_element_type=F32
        )
        both = packed.astype(BF16)
        for h in range(2):
            for g in range(2):
                x[h, g, 0, 0, :, at] = both[h * rows + g * hr : h * rows + (g + 1) * hr]
        prod = packed[0:rows] * router[:, at].astype(F32)
        prod += packed[rows : 2 * rows] * router[:, pl.ds(half + c, w)].astype(F32)
        s = score[...]
        for t in range(w // 128):
            s = s + prod[:, t * 128 : (t + 1) * 128]
        score[...] = s

    def blk(h, g, da, db, c, w):
        if h == 1:
            da, db = db, da
        return x.at[h, g, da, db, :, pl.ds(c, w)]

    SETS = (0, NEAR, 3)

    def second(i, n):
        g, c, w = GATHERS[i]
        da = SETS[n]
        s, r = ag_send.at[1], ag_p2.at[i, n]
        for h in range(2):
            send(blk(h, g, da, 0, c, w), blk(h, g, da, 1, c, w), s, r, near(h, "b", 1))
            send(blk(h, g, da, 0, c, w), blk(h, g, da, 2, c, w), s, r, near(h, "b", -1))

    def own(i):
        g, c, w = GATHERS[i]
        s, r = ag_send.at[0], ag_p1.at[i, 0]
        for h in range(2):
            send(blk(h, g, 0, 0, c, w), blk(h, g, 1, 0, c, w), s, r, near(h, "a", 1))
            send(blk(h, g, 0, 0, c, w), blk(h, g, 2, 0, c, w), s, r, near(h, "a", -1))

    def own2(i):
        second(i, 0)

    def first_hop(i):
        g, c, w = GATHERS[i]
        hw = w // 2
        s, r = ag_send.at[0], ag_p1.at[i, 1]
        settle(x.at[0, g, 0, :, :, pl.ds(c, w)], ag_p1.at[i, 0])
        for h in range(2):
            send(blk(h, g, 1, 0, c, hw), blk(h, g, 3, 0, c, hw), s, r, near(h, "a", 1))
            send(blk(h, g, 2, 0, c + hw, hw), blk(h, g, 3, 0, c + hw, hw), s, r, near(h, "a", -1))
        second(i, 1)

    def second_hop(i):
        g, c, w = GATHERS[i]
        settle(x.at[0, g, 0, pl.ds(0, 2), :, pl.ds(c, w)], ag_p1.at[i, 1])
        second(i, 2)

    def forward(i, n):
        g, c, w = GATHERS[i]
        hw = w // 2
        da = SETS[n]
        s, r = ag_send.at[1], ag_end.at[i]
        settle(x.at[0, g, pl.ds(0, 2 if n == 1 else 1), :, :, pl.ds(c, w)], ag_p2.at[i, n])
        for h in range(2):
            send(blk(h, g, da, 1, c, hw), blk(h, g, da, 3, c, hw), s, r, near(h, "b", 1))
            send(blk(h, g, da, 2, c + hw, hw), blk(h, g, da, 3, c + hw, hw), s, r, near(h, "b", -1))

    def gathered(i):
        g, c, w = GATHERS[i]
        if i == 0:
            settle(w1, local_sem.at[1])
        settle(x.at[0, g, pl.ds(0, 2), :, :, pl.ds(c, w)], ag_end.at[i])
        for h in range(2):
            v = jnp.dot(
                x[h, g, :, :, :, pl.ds(c, w)].reshape(slots, w),
                w1[pl.ds(h * half + c, w), :],
                preferred_element_type=F32,
            )
            if c == 0 and h == 0:
                acc[g] = v
            else:
                acc[g] += v

    def hide(g):
        gv, uv = acc[g, :, 0:width], acc[g, :, width : 2 * width]
        hid[g] = (gv / (1.0 + jnp.exp(-gv)) * uv).astype(BF16)
        if g == 0:
            settle(w2, local_sem.at[2])

    def add(ref, index, more):
        ref[index] = (ref[index].astype(F32) + more.astype(F32)).astype(BF16)

    def multiply(i):
        g, c, w = REDUCES[i]
        hw = w // 2
        lo, hi = pl.ds(c, hw), pl.ds(c + hw, hw)
        for h in range(2):
            for t in range(c, c + w, 256):
                v = jnp.dot(hid[g], w2[:, pl.ds(h * half + t, 256)], preferred_element_type=F32)
                v = v.astype(BF16).reshape(SIDE, SIDE, hr, 256)
                if h == 1:
                    part[h, g, :, :, :, pl.ds(t, 256)] = v
                else:
                    for da in range(SIDE):
                        for db in range(SIDE):
                            part[h, g, db, da, :, pl.ds(t, 256)] = v[da, db]
            s = rs_send.at[0]
            send(part.at[h, g, 3, :, :, lo], r1.at[h, g, :, :, lo], s, rs_p1.at[i, 0], near(h, "b", -1))
            send(part.at[h, g, 3, :, :, hi], r1.at[h, g, :, :, hi], s, rs_p1.at[i, 0], near(h, "b", 1))
            send(part.at[h, g, 1, :, :, hi], f1.at[h, g, 0, :, :, hi], s, rs_p1.at[i, 1], near(h, "b", -1))
            send(part.at[h, g, 2, :, :, lo], f1.at[h, g, 1, :, :, lo], s, rs_p1.at[i, 1], near(h, "b", 1))

    def first_on(i):
        g, c, w = REDUCES[i]
        hw = w // 2
        lo, hi = pl.ds(c, hw), pl.ds(c + hw, hw)
        s = rs_send.at[0]
        settle(r1.at[:, g, :, :, pl.ds(c, w)], rs_p1.at[i, 0])
        for h in range(2):
            add(part, (h, g, 1, slice(None), slice(None), lo), r1[h, g, :, :, lo])
            send(part.at[h, g, 1, :, :, lo], f1.at[h, g, 0, :, :, lo], s, rs_p1.at[i, 1], near(h, "b", -1))
            add(part, (h, g, 2, slice(None), slice(None), hi), r1[h, g, :, :, hi])
            send(part.at[h, g, 2, :, :, hi], f1.at[h, g, 1, :, :, hi], s, rs_p1.at[i, 1], near(h, "b", 1))

    def first_end(i):
        g, c, w = REDUCES[i]
        hw = w // 2
        at, lo, hi = pl.ds(c, w), pl.ds(c, hw), pl.ds(c + hw, hw)
        settle(f1.at[:, g, :, :, :, at], rs_p1.at[i, 1])
        for h in range(2):
            red[h, g, :, :, at] = (
                part[h, g, 0, :, :, at].astype(F32)
                + f1[h, g, 0, :, :, at].astype(F32)
                + f1[h, g, 1, :, :, at].astype(F32)
            ).astype(BF16)
            s = rs_send.at[1]
            send(red.at[h, g, 3, :, lo], r2.at[h, g, :, lo], s, rs_p2.at[i, 0], near(h, "a", -1))
            send(red.at[h, g, 3, :, hi], r2.at[h, g, :, hi], s, rs_p2.at[i, 0], near(h, "a", 1))
            send(red.at[h, g, 1, :, hi], f2.at[h, g, 0, :, hi], s, rs_p2.at[i, 1], near(h, "a", -1))
            send(red.at[h, g, 2, :, lo], f2.at[h, g, 1, :, lo], s, rs_p2.at[i, 1], near(h, "a", 1))

    def second_on(i):
        g, c, w = REDUCES[i]
        hw = w // 2
        lo, hi = pl.ds(c, hw), pl.ds(c + hw, hw)
        s = rs_send.at[1]
        settle(r2.at[:, g, :, pl.ds(c, w)], rs_p2.at[i, 0])
        for h in range(2):
            add(red, (h, g, 1, slice(None), lo), r2[h, g, :, lo])
            send(red.at[h, g, 1, :, lo], f2.at[h, g, 0, :, lo], s, rs_p2.at[i, 1], near(h, "a", -1))
            add(red, (h, g, 2, slice(None), hi), r2[h, g, :, hi])
            send(red.at[h, g, 2, :, hi], f2.at[h, g, 1, :, hi], s, rs_p2.at[i, 1], near(h, "a", 1))

    def second_end(i):
        g, c, w = REDUCES[i]
        hw = w // 2
        at, lo, hi = pl.ds(c, w), pl.ds(c, hw), pl.ds(c + hw, hw)
        weight = jax.nn.sigmoid(jnp.sum(score[g * hr : (g + 1) * hr, :], axis=1, keepdims=True))
        settle(f2.at[:, g, :, :, at], rs_p2.at[i, 1])
        for h in range(2):
            v = red[h, g, 0, :, at].astype(F32) + f2[h, g, 0, :, at].astype(F32) + f2[h, g, 1, :, at].astype(F32)
            res[h, g * hr : (g + 1) * hr, at] = (v * weight).astype(BF16)

    def give_back(i):
        c, w = RETURNS[i]
        at = pl.ds(c, w)
        both = jnp.concatenate([res[0, :, at], res[1, :, at]], axis=0)
        back = jnp.dot(unpack_m, both, preferred_element_type=F32)
        ro[:, :, at] = back.astype(BF16).reshape(GROUP, 16, w)
        for o in (4, 3, 5, 2, 6, 7, 1):
            to = lax.rem(e + o, GROUP)
            send(ro.at[to, :, at], rr.at[e, :, at], ret_send.at[0], ret_recv.at[i], other(o))
        pltpu.make_async_copy(ro.at[e, :, at], rr.at[e, :, at], local_sem.at[8]).start()

    def finish(i):
        c, w = RETURNS[i]
        settle(rr.at[pl.ds(0, GROUP - 1), :, pl.ds(c, w)], ret_recv.at[i])

    norm(0)
    unpack_m = pack_matrices()
    load_weights()
    norm(1)
    norm(2)
    clear()
    packing(0)
    own(0)
    own2(0)
    packing(1)
    own(4)
    own(1)
    own2(4)
    own2(1)
    first_hop(0)
    norm(3)
    packing(2)
    own(2)
    forward(0, 0)
    own2(2)
    own(5)
    first_hop(4)
    first_hop(1)
    second_hop(0)
    first_hop(2)
    first_hop(5)
    forward(2, 0)
    packing(3)
    own2(3)
    forward(1, 1)
    own(3)
    second_hop(2)
    own2(6)
    second_hop(1)
    own2(5)
    own(7)
    own(6)
    forward(3, 0)
    forward(0, 2)
    forward(0, 1)
    first_hop(3)
    forward(2, 2)
    first_hop(7)
    forward(1, 2)
    second_hop(4)
    forward(1, 0)
    first_hop(6)
    own2(7)
    second_hop(3)
    forward(2, 1)
    second_hop(7)
    second_hop(5)
    forward(5, 0)
    gathered(0)
    second_hop(6)
    forward(3, 1)
    forward(3, 2)
    gathered(1)
    forward(7, 0)
    forward(4, 1)
    forward(5, 2)
    forward(7, 1)
    forward(6, 0)
    gathered(2)
    forward(6, 1)
    forward(7, 2)
    forward(4, 2)
    forward(6, 2)
    forward(4, 0)
    forward(5, 1)
    gathered(3)
    hide(0)
    multiply(3)
    multiply(2)
    multiply(0)
    multiply(1)
    gathered(4)
    gathered(5)
    gathered(6)
    gathered(7)
    hide(1)
    multiply(4)
    multiply(5)
    first_on(4)
    first_on(0)
    multiply(6)
    first_on(1)
    first_on(5)
    first_on(6)
    first_end(0)
    first_end(4)
    multiply(7)
    first_end(5)
    first_on(2)
    second_on(4)
    second_on(0)
    first_on(3)
    first_end(1)
    first_on(7)
    second_on(5)
    first_end(6)
    second_end(4)
    first_end(2)
    second_on(1)
    first_end(3)
    second_end(0)
    give_back(0)
    first_end(7)
    second_end(5)
    second_on(6)
    second_on(2)
    second_end(1)
    give_back(1)
    second_on(3)
    second_on(7)
    second_end(6)
    second_end(2)
    give_back(2)
    second_end(3)
    second_end(7)
    give_back(3)
    finish(1)
    finish(0)
    finish(2)
    finish(3)

    settle(x.at[:, :, 0, pl.ds(0, 3)], ag_send.at[0])
    settle(x.at[:, :, pl.ds(0, 3)], ag_send.at[1])
    settle(part.at[:, :, pl.ds(0, 3)], rs_send.at[0])
    settle(red.at[:, :, pl.ds(0, 3)], rs_send.at[1])
    settle(so.at[pl.ds(0, GROUP - 1)], a2a_send.at[0])
    settle(ro.at[pl.ds(0, GROUP - 1)], ret_send.at[0])
    settle(ro.at[0], local_sem.at[8])
    put_copy.wait()


def add_returned(tokens, returned, put_in, out, tok, back, put, ob, load_sem, store_sem, put_sem):
    ntok, half = tokens.shape[0], tokens.shape[1] // 2
    w = half // PIECES
    put_copy = pltpu.make_async_copy(put_in, put, put_sem.at[0])
    put_copy.start()
    loads, stores = [], []
    for i in range(PIECES):
        at = pl.ds(i * w, w)
        row = [pltpu.make_async_copy(returned.at[:, :, at], back.at[:, :, at], load_sem.at[i, 2])]
        for h in range(2):
            there = pl.ds(h * half + i * w, w)
            row.append(pltpu.make_async_copy(tokens.at[:, there], tok.at[h, :, at], load_sem.at[i, h]))
        for cp in row:
            cp.start()
        loads.append(row)
    put_copy.wait()
    for i in range(PIECES):
        at = pl.ds(i * w, w)
        for cp in loads[i]:
            cp.wait()
        v = jnp.dot(put[...], back[:, :, at].reshape(GROUP * 16, w), preferred_element_type=F32)
        t = tok[:, :, at].reshape(2 * ntok, w).astype(F32)
        ob[:, :, at] = (t + v).astype(BF16).reshape(2, ntok, w)
        for h in range(2):
            cp = pltpu.make_async_copy(ob.at[h, :, at], out.at[:, pl.ds(h * half + i * w, w)], store_sem.at[i, h])
            cp.start()
            stores.append(cp)
    for cp in stores:
        cp.wait()


def shards(tokens, modality, norm_gain, picks, counts, router, gate_weight, up_weight, down_weight):
    ntok, d = tokens.shape
    half = d // 2
    hidden = gate_weight.shape[2]
    rows = GROUP * picks.shape[2] // 2
    hr = rows // 2
    anywhere = pl.BlockSpec(memory_space=pl.ANY)
    dma = pltpu.SemaphoreType.DMA
    slots = hr * SIDE * SIDE
    ne, ng, nr, nb = len(EXCHANGES), len(GATHERS), len(REDUCES), len(RETURNS)
    returned, put = pl.pallas_call(
        kernel,
        name="expert_layer",
        out_shape=(
            jax.ShapeDtypeStruct((GROUP, 16, half), BF16),
            jax.ShapeDtypeStruct((2 * ntok, GROUP * 16), BF16),
        ),
        in_specs=[anywhere] * 8,
        out_specs=(anywhere, anywhere),
        scratch_shapes=[
            pltpu.VMEM(norm_gain.shape, F32),
            pltpu.VMEM(picks.shape, jnp.int32),
            pltpu.VMEM(counts.shape, jnp.int32),
            pltpu.VMEM(router.shape, BF16),
            pltpu.VMEM((2, ntok, half), BF16),
            pltpu.VMEM((d, 2 * hidden), BF16),
            pltpu.VMEM((hidden, d), BF16),
            pltpu.VMEM((GROUP, 16, half), BF16),
            pltpu.VMEM((GROUP, 16, half), BF16),
            pltpu.VMEM((2, 2, SIDE, SIDE, hr, half), BF16),
            pltpu.VMEM((2, slots, 2 * hidden), F32),
            pltpu.VMEM((2, slots, hidden), BF16),
            pltpu.VMEM((2, 2, SIDE, SIDE, hr, half), BF16),
            pltpu.VMEM((2, 2, SIDE, hr, half), BF16),
            pltpu.VMEM((2, 2, 2, SIDE, hr, half), BF16),
            pltpu.VMEM((2, 2, SIDE, hr, half), BF16),
            pltpu.VMEM((2, 2, hr, half), BF16),
            pltpu.VMEM((2, 2, 2, hr, half), BF16),
            pltpu.VMEM((2, rows, half), BF16),
            pltpu.VMEM((GROUP, 16, half), BF16),
            pltpu.VMEM((rows, 128), F32),
            pltpu.VMEM((2 * ntok + 2 * rows, GROUP * 16), BF16),
            dma((9,)),
            dma((1,)),
            dma((ne,)),
            dma((2,)),
            dma((ng, 2)),
            dma((ng, 3)),
            dma((ng,)),
            dma((2,)),
            dma((nr, 2)),
            dma((nr, 2)),
            dma((1,)),
            dma((nb,)),
        ],
        compiler_params=pltpu.CompilerParams(
            collective_id=0, has_side_effects=True, vmem_limit_bytes=56 * 2**20
        ),
        cost_estimate=pl.CostEstimate(
            flops=12 * slots * d * hidden, bytes_accessed=16 * 2**20, transcendentals=2 * slots * hidden
        ),
    )(tokens, norm_gain, picks, counts, router, gate_weight, up_weight, down_weight)
    return pl.pallas_call(
        add_returned,
        name="add_returned",
        out_shape=jax.ShapeDtypeStruct((ntok, d), BF16),
        in_specs=[anywhere] * 3,
        out_specs=anywhere,
        scratch_shapes=[
            pltpu.VMEM((2, ntok, half), BF16),
            pltpu.VMEM((GROUP, 16, half), BF16),
            pltpu.VMEM((2 * ntok, GROUP * 16), BF16),
            pltpu.VMEM((2, ntok, half), BF16),
            dma((PIECES, 3)),
            dma((PIECES, 2)),
            dma((1,)),
        ],
        compiler_params=pltpu.CompilerParams(vmem_limit_bytes=57 * 2**20),
        cost_estimate=pl.CostEstimate(
            flops=4 * ntok * GROUP * 16 * half, bytes_accessed=5 * ntok * d, transcendentals=0
        ),
    )(tokens, returned, put)


def solution(mesh):
    placed = (
        P(("dp", "expert"), None),
        P(("dp", "expert")),
        P(),
        P(None, ("dp", "expert"), None),
        P(),
        P("expert", None),
        P("expert", None, "dp"),
        P("expert", None, "dp"),
        P("expert", "dp", None),
    )
    return jax.shard_map(
        shards, mesh=mesh, in_specs=placed, out_specs=P(("dp", "expert"), None), check_vma=False
    )
```
